128 devices in a mesh: section: 2 (over core), node: 16 (over y, x), local: 4 (over z).
Axes of the slice: x: 4, y: 4, z: 4, core: 2. Of those that a mesh axis runs over, the one named last changes fastest.
Arguments:
- grad_out: bfloat16 [4096, 7168], P(('section', 'node'), 'local'), may hold values from -6 to 6
- node_ids: int32 [4096, 4], P(('section', 'node')), may hold values from 0 to 15, as said below
- expert_ids: int32 [4096, 6], P(('section', 'node')), may hold values from 0 to 31, as said below
- gate_probs: float32 [4096, 6], P(('section', 'node')), may hold values from 0.05 to 0.5
- gate_pre: bfloat16 [64, 1024, 1024], P(('section', 'node'), None, 'local'), may hold values from -6 to 6
- up_pre: bfloat16 [64, 1024, 1024], P(('section', 'node'), None, 'local'), may hold values from -6 to 6
- gate_weight: bfloat16 [64, 7168, 1024], P(('section', 'node'), 'local'), may hold values from -0.0625 to 0.0625
- up_weight: bfloat16 [64, 7168, 1024], P(('section', 'node'), 'local'), may hold values from -0.0625 to 0.0625
- down_weight: bfloat16 [64, 1024, 7168], P(('section', 'node'), None, 'local'), may hold values from -0.1875 to 0.1875
Outputs:
- handed: bfloat16 [4096, 7168], P(('section', 'node'), 'local')
- prob_grad: float32 [4096, 6], P(('section', 'node'))
The draws below stay inside these ranges and needn't reach their ends.
Inputs may be any that keep to these rules, and one draw needn't show every extreme that they name: `node_ids`: each row names 4 different node groups of its section. Of the 128 tokens of one block, at most 64 name any one node group, and in each section one node group is named by exactly 64 tokens of every block. `expert_ids`: each row names 6 different experts of its section; expert e belongs to node group e // 2, each named expert belongs to one of the row's node groups, and each of the row's node groups holds at least one named expert.
All inputs are finite; a program needn't handle non-finite values.
Results may differ from the reference program's by a relative error of at most 0.02.
Values may be sent and summed in bfloat16 or wider, within the bound.
A program may use at most 128 MiB of HBM per device.

```python
import math
import jax
import jax.numpy as jnp
from jax import lax

D = 7168
FF = 1024
TOK_NODE = 128
E_NODE = 2
TOPK = 6
NODES_TOK = 4
CAPN = 64
TOKENS = 2048
EXPERTS = 32
ROWS_NODE = 1024
N_SECTION = 2
N_NODE = 16
N_LOCAL = 4


def route_tables(key):
    blocks = N_SECTION * N_NODE
    group_size = N_NODE // NODES_TOK
    key_favor, key_coin, key_other, key_order, key_score, key_keep, key_column = jax.random.split(key, 7)
    favorite = jax.random.randint(key_favor, (NODES_TOK,), 0, group_size, dtype=jnp.int32)
    coin = jax.random.randint(key_coin, (blocks, NODES_TOK), 0, 2, dtype=jnp.int32)
    coin = coin.at[:, 0].set(0)
    other = jax.random.randint(key_other, (blocks, NODES_TOK), 0, group_size, dtype=jnp.int32)
    hottest = jnp.where(coin == 0, favorite[None, :], other)
    order_keys = jax.random.split(key_order, blocks * NODES_TOK)
    orders = jax.vmap(lambda one_key: jax.random.permutation(one_key, TOK_NODE))(order_keys)
    ranks = jnp.argsort(orders, axis=1).astype(jnp.int32).reshape(blocks, NODES_TOK, TOK_NODE)
    spread = max(TOK_NODE - CAPN, 1)
    others = jnp.maximum(ranks - CAPN, 0) * max(group_size - 1, 1) // spread
    others = others + (others >= hottest[:, :, None]).astype(jnp.int32)
    member = jnp.where(ranks < CAPN, hottest[:, :, None], others)
    group_base = (jnp.arange(NODES_TOK, dtype=jnp.int32) * group_size)[None, :, None]
    node_ids = jnp.transpose(member + group_base, (0, 2, 1)).reshape(blocks * TOK_NODE, NODES_TOK)
    column_score = jax.random.randint(key_column, (blocks * TOK_NODE, NODES_TOK), 0, 1024, dtype=jnp.int32)
    column_score = column_score * NODES_TOK + jnp.arange(NODES_TOK, dtype=jnp.int32)[None, :]
    column_order = jnp.argsort(column_score, axis=1).astype(jnp.int32)
    node_ids = jnp.take_along_axis(node_ids, column_order, axis=1)
    candidates = NODES_TOK * E_NODE
    score = jax.random.randint(key_score, (blocks * TOK_NODE, candidates), 0, 1024, dtype=jnp.int32)
    keep = jax.random.randint(key_keep, (blocks * TOK_NODE, NODES_TOK), 0, E_NODE, dtype=jnp.int32)
    certain = (jnp.arange(E_NODE, dtype=jnp.int32)[None, None, :] == keep[:, :, None]).reshape(blocks * TOK_NODE, candidates)
    score = (score + certain.astype(jnp.int32) * 4096) * candidates + jnp.arange(candidates, dtype=jnp.int32)[None, :]
    picked = jnp.argsort(-score, axis=1)[:, :TOPK].astype(jnp.int32)
    local_expert = picked % E_NODE
    node_column = picked // E_NODE
    expert_ids = jnp.take_along_axis(node_ids, node_column, axis=1) * E_NODE + local_expert
    return (node_ids.astype(jnp.int32), expert_ids.astype(jnp.int32))


def draw_node_ids(key, part):
    tables = route_tables(key)
    return tables[0]


def draw_expert_ids(key, part):
    tables = route_tables(key)
    return tables[1]


def levels(own_key, extent, cuts, smallest, largest):
    gain = 1.0
    for dim, parts in cuts:
        draws = jax.random.uniform(jax.random.fold_in(jax.random.fold_in(own_key, 6), dim), (parts,), jnp.float32, smallest / len(cuts), largest / len(cuts))
        gain = gain * jnp.repeat(jnp.exp(draws), extent[dim] // parts).reshape((-1,) + (1,) * (len(extent) - 1 - dim))
    return gain


def gaussian(rng, dims, scale, bound, cuts=(), kind=jnp.bfloat16):
    loudness = levels(rng, dims, cuts, -0.22, 0.18) if cuts else 1.0
    drawn = jax.random.normal(rng, dims, jnp.float32) * scale * loudness
    return jnp.minimum(jnp.maximum(drawn, -bound), bound).astype(kind)


def setup_inputs(seed: int = 0) -> dict:
    key_of = jax.random.split(jax.random.key(seed), 10)
    return {
        "grad_out": gaussian(key_of[0], (N_SECTION * TOKENS, D), 1.0, 6.0, ((0, 32), (1, 4))),
        "node_ids": draw_node_ids(jax.random.fold_in(key_of[9], 71), 0),
        "expert_ids": draw_expert_ids(jax.random.fold_in(key_of[9], 71), 0),
        "gate_probs": jnp.clip(jnp.exp(math.log(0.5) - 2.3025851 * jax.random.uniform(key_of[3], (N_SECTION * TOKENS, TOPK), jnp.float32) ** levels(key_of[3], (N_SECTION * TOKENS, TOPK), ((0, 32),), -0.2, 0.2)), 0.05, 0.5),
        "gate_pre": gaussian(key_of[4], (N_SECTION * EXPERTS, ROWS_NODE, FF), 1.0, 6.0, ((0, 32), (2, 4))),
        "up_pre": gaussian(key_of[5], (N_SECTION * EXPERTS, ROWS_NODE, FF), 1.0, 6.0, ((0, 32), (2, 4))),
        "gate_weight": gaussian(key_of[6], (N_SECTION * EXPERTS, D, FF), D ** -0.5, 0.0625, ((0, 32), (1, 4))),
        "up_weight": gaussian(key_of[7], (N_SECTION * EXPERTS, D, FF), D ** -0.5, 0.0625, ((0, 32), (1, 4))),
        "down_weight": gaussian(key_of[8], (N_SECTION * EXPERTS, FF, D), FF ** -0.5, 0.1875, ((0, 32), (2, 4))),
    }


def silu_backward(raw_grad, weight_rows, gate_pre, up_pre):
    gate_value = gate_pre.astype(jnp.float32)
    up_value = up_pre.astype(jnp.float32)
    sigmoid_gate = jax.nn.sigmoid(gate_value)
    active = gate_value * sigmoid_gate
    prob_part = jnp.sum(raw_grad * active * up_value, axis=2)
    scaled = raw_grad * weight_rows[:, :, None]
    gate_grad = (scaled * up_value * sigmoid_gate * (1.0 + gate_value * (1.0 - sigmoid_gate))).astype(jnp.bfloat16)
    up_grad = (scaled * active).astype(jnp.bfloat16)
    return prob_part, gate_grad, up_grad


def routing_rows(node_ids):
    node_range = jnp.arange(N_NODE, dtype=jnp.int32)
    member = jnp.any(node_ids[:, :, None] == node_range[None, None, :], axis=1).astype(jnp.int32)
    blocked = member.reshape(N_NODE, TOK_NODE, N_NODE)
    position = (jnp.cumsum(blocked, axis=1, dtype=jnp.int32) - blocked).reshape(TOKENS, N_NODE)
    anchor = (jnp.arange(TOKENS, dtype=jnp.int32) // TOK_NODE)[:, None]
    row_table = jnp.where(member > 0, anchor * CAPN + position, ROWS_NODE)
    return row_table.astype(jnp.int32)


def one_section(grad_out, node_ids, expert_ids, gate_probs, gate_pre, up_pre, gate_weight, up_weight, down_weight):
    row_table = routing_rows(node_ids)
    slice_width = D // N_LOCAL

    def per_node(carry, inputs):
        input_grad, prob_grad = carry
        node_index, gate_saved, up_saved, gate_block, up_block, down_block = inputs
        slot_rows = row_table[:, node_index]
        arrived = jnp.zeros((ROWS_NODE + 1, D), jnp.bfloat16).at[slot_rows].set(grad_out)[:ROWS_NODE]
        target = node_index * E_NODE + jnp.arange(E_NODE, dtype=jnp.int32)
        matched = expert_ids[:, :, None] == target[None, None, :]
        token_mass = jnp.sum(jnp.where(matched, gate_probs[:, :, None], 0.0), axis=1)
        mass_rows = jnp.zeros((ROWS_NODE + 1, E_NODE), jnp.float32).at[slot_rows].set(token_mass)[:ROWS_NODE]
        mass_half = lax.optimization_barrier(mass_rows.astype(jnp.bfloat16))
        weight_rows = mass_half.astype(jnp.float32).T
        pieces = arrived.astype(jnp.float32).reshape(ROWS_NODE, N_LOCAL, slice_width)
        down_slices = down_block.astype(jnp.float32).reshape(E_NODE, FF, N_LOCAL, slice_width)
        partial_value = jnp.einsum('rld,efld->lerf', pieces, down_slices)
        partial_half = lax.optimization_barrier(partial_value.astype(jnp.bfloat16))
        raw_grad = jnp.sum(partial_half.astype(jnp.float32), axis=0)
        prob_rows, gate_grad, up_grad = silu_backward(raw_grad, weight_rows, gate_saved, up_saved)
        prob_half = lax.optimization_barrier(prob_rows.astype(jnp.bfloat16))
        prob_rows = prob_half.astype(jnp.float32)
        returned = jnp.einsum('erf,edf->rd', gate_grad.astype(jnp.float32), gate_block.astype(jnp.float32))
        returned = returned + jnp.einsum('erf,edf->rd', up_grad.astype(jnp.float32), up_block.astype(jnp.float32))
        returned_half = lax.optimization_barrier(returned.astype(jnp.bfloat16))
        returned = returned_half.astype(jnp.float32)
        returned_ext = jnp.concatenate([returned, jnp.zeros((1, D), jnp.float32)], axis=0)
        input_grad = input_grad + returned_ext[slot_rows]
        prob_ext = jnp.concatenate([prob_rows.T, jnp.zeros((1, E_NODE), jnp.float32)], axis=0)
        picked = prob_ext[slot_rows]
        prob_grad = prob_grad + jnp.sum(jnp.where(matched, picked[:, None, :], 0.0), axis=2)
        return (input_grad, prob_grad), None

    def by_node(array):
        return array.reshape((N_NODE, E_NODE) + array.shape[1:])

    inputs = (jnp.arange(N_NODE, dtype=jnp.int32), by_node(gate_pre), by_node(up_pre),
              by_node(gate_weight), by_node(up_weight), by_node(down_weight))
    start = (jnp.zeros((TOKENS, D), jnp.float32), jnp.zeros((TOKENS, TOPK), jnp.float32))
    (input_grad, prob_grad), unused = lax.scan(per_node, start, inputs)
    return input_grad.astype(jnp.bfloat16), prob_grad


def reference(grad_out, node_ids, expert_ids, gate_probs, gate_pre, up_pre, gate_weight, up_weight, down_weight):
    handed_parts = []
    prob_parts = []
    for section_index in range(N_SECTION):
        token_lo = section_index * TOKENS
        expert_lo = section_index * EXPERTS
        token_part = slice(token_lo, token_lo + TOKENS)
        expert_part = slice(expert_lo, expert_lo + EXPERTS)
        input_grad, prob_grad = one_section(grad_out[token_part], node_ids[token_part], expert_ids[token_part],
                                          gate_probs[token_part], gate_pre[expert_part], up_pre[expert_part],
                                          gate_weight[expert_part], up_weight[expert_part], down_weight[expert_part])
        handed_parts.append(input_grad)
        prob_parts.append(prob_grad)
    handed_parts = handed_parts[1:] + handed_parts[:1]
    return jnp.concatenate(handed_parts, axis=0), jnp.concatenate(prob_parts, axis=0)
```

```python
import functools

import jax
import jax.numpy as jnp
from jax import lax
from jax.experimental import pallas as pl
from jax.experimental.pallas import tpu as pltpu
from jax.sharding import PartitionSpec as P

MESH = pl.DeviceIdType.MESH
SIDE = 4
NODES = 16
CAP = 64
UNIT = 16
TILE = 128
EXTRA = 128
CHUNKS = (8, 8, 16, 16, 8, 8)


def offset(o):
    half = o // 8
    rest = o % 8
    dy = rest // 2
    dx = (2 * (rest % 2) + dy % 2 + half) % SIDE
    return dy, dx


def nt_dot(a, b):
    return lax.dot_general(a, b, (((1,), (1,)), ((), ())), preferred_element_type=jnp.float32)


def kernel(
    x_ref,
    nodes_ref,
    experts_ref,
    probs_ref,
    gate_pre_ref,
    up_pre_ref,
    gate_w_ref,
    up_w_ref,
    down_w_ref,
    handed_ref,
    prob_ref,
    gate_pre,
    up_pre,
    gate_w,
    up_w,
    down_w,
    x_ext,
    sel,
    sel_other,
    out_rows,
    in_rows,
    part,
    rs_far,
    rs_near,
    grads,
    ret_rows,
    back_rows,
    acc,
    mine,
    total,
    load_sem,
    disp_send,
    disp_recv,
    sel_send,
    sel_recv,
    rs_send,
    rs_far_recv,
    rs_near_recv,
    ag_send,
    ag_recv,
    ag_far_recv,
    ret_send,
    ret_recv,
    tok_send,
    tok_recv,
):
    s = lax.axis_index("section")
    n = lax.axis_index("node")
    z = lax.axis_index("local")
    other = 1 - s
    my, mx = n // SIDE, n % SIDE
    up = lax.rem(z + 1, SIDE)
    down = lax.rem(z + 3, SIDE)
    tokens, width = x_ref.shape
    full = width + EXTRA
    rows_node = gate_pre.shape[1]
    hidden = gate_pre.shape[2]

    def node_plus(o):
        dy, dx = offset(o)
        return ((my + dy) % SIDE) * SIDE + (mx + dx) % SIDE

    def node_minus(o):
        dy, dx = offset(o)
        return ((my + SIDE - dy) % SIDE) * SIDE + (mx + SIDE - dx) % SIDE

    def rows_of(start, count):
        return pl.ds(pl.multiple_of(start, UNIT), count)

    def quarter(index):
        return pl.ds(pl.multiple_of(index * hidden, hidden), hidden)

    loads = [
        pltpu.make_async_copy(src, dst, load_sem.at[i])
        for i, (src, dst) in enumerate(
            (
                (down_w_ref, down_w),
                (gate_pre_ref, gate_pre),
                (up_pre_ref, up_pre),
                (gate_w_ref, gate_w),
                (up_w_ref, up_w),
            )
        )
    ]
    loads[0].start()

    barrier = pltpu.get_barrier_semaphore()

    def greet(section, node, local):
        pl.semaphore_signal(
            barrier,
            inc=1,
            device_id={"section": section, "node": node, "local": local},
            device_id_type=MESH,
        )

    greet(s, n, up)
    greet(s, n, down)
    for k in range(1, SIDE):
        greet(other, n, (z + k) % SIDE)

    @pl.loop(1, NODES)
    def _(o):
        greet(s, node_plus(o), z)

    @pl.loop(0, NODES)
    def _(o):
        greet(other, node_plus(o), z)

    for load in loads[1:]:
        load.start()

    lane = lax.broadcasted_iota(jnp.int32, (tokens, EXTRA), 1)
    mass = jnp.zeros((tokens, EXTRA), jnp.float32)
    for k in range(experts_ref.shape[1]):
        mass = mass + jnp.where(lane == experts_ref[:, k : k + 1], probs_ref[:, k : k + 1], 0.0)
    x_ext[:, width:] = mass.astype(jnp.bfloat16)
    x_ext[:, :width] = x_ref[...]

    before = (
        lax.broadcasted_iota(jnp.int32, (tokens, tokens), 1)
        < lax.broadcasted_iota(jnp.int32, (tokens, tokens), 0)
    )
    before = jnp.where(before, 1.0, 0.0).astype(jnp.bfloat16)

    pl.semaphore_wait(barrier, 2 + (SIDE - 1) + (NODES - 1) + NODES)

    @pl.loop(0, rows_node // TILE)
    def _(t):
        column = lax.broadcasted_iota(jnp.int32, (tokens, TILE), 1) + t * TILE
        u = column >> 4
        o = u & 15
        rest = o & 7
        dy = rest >> 1
        dx = (2 * (rest & 1) + (dy & 1) + (o >> 3)) & 3
        node = ((my + dy) & 3) * SIDE + ((mx + dx) & 3)
        slot = (u >> 4) * UNIT + (column & 15)
        member = nodes_ref[:, 0:1] == node
        for k in range(1, nodes_ref.shape[1]):
            member = member | (nodes_ref[:, k : k + 1] == node)
        member = jnp.where(member, 1.0, 0.0)
        position = jnp.dot(
            before, member.astype(jnp.bfloat16), preferred_element_type=jnp.float32
        )
        chosen = jnp.where(position == slot.astype(jnp.float32), member, 0.0)
        sel[t] = chosen.astype(jnp.bfloat16)
        picked = jnp.dot(
            chosen.T.astype(jnp.bfloat16), x_ext[...], preferred_element_type=jnp.float32
        ).astype(jnp.bfloat16)
        first = rows_of(t * TILE, TILE)
        out_rows[first, :] = picked

        @pl.when(t % 2 == 0)
        def _():
            in_rows[rows_of(t * TILE, UNIT), :] = picked[:UNIT]

        @pl.loop(1 - t % 2, TILE // UNIT)
        def _(i):
            rows = rows_of(t * TILE + i * UNIT, UNIT)
            pltpu.make_async_remote_copy(
                src_ref=out_rows.at[rows],
                dst_ref=in_rows.at[rows],
                send_sem=disp_send,
                recv_sem=disp_recv.at[t],
                device_id={"section": s, "node": node_plus((t % 2) * 8 + i), "local": z},
                device_id_type=MESH,
            ).start()

    sel_copy = pltpu.make_async_remote_copy(
        src_ref=sel,
        dst_ref=sel_other,
        send_sem=sel_send,
        recv_sem=sel_recv,
        device_id={"section": other, "node": n, "local": z},
        device_id_type=MESH,
    )
    sel_copy.start()

    starts = [UNIT * sum(CHUNKS[:c]) for c in range(len(CHUNKS))]
    sizes = [UNIT * count for count in CHUNKS]

    def along_z(src, dst, send_sem, recv_sem, local):
        pltpu.make_async_remote_copy(
            src_ref=src,
            dst_ref=dst,
            send_sem=send_sem,
            recv_sem=recv_sem,
            device_id={"section": s, "node": n, "local": local},
            device_id_type=MESH,
        ).start()

    def landed(ref, sem):
        pltpu.make_async_copy(ref, ref, sem).wait()

    def multiply_down(c):
        begin, count = starts[c], sizes[c]
        rows = pl.ds(begin, count)
        for t in range(begin // TILE, (begin + count) // TILE):
            if t % 2 == 0:
                landed(in_rows.at[pl.ds(t * TILE + UNIT, TILE - UNIT)], disp_recv.at[t])
            else:
                landed(in_rows.at[pl.ds(t * TILE, TILE)], disp_recv.at[t])
        if c == 0:
            loads[0].wait()

        def products(first, last, step_of):
            @pl.loop(2 * first, 2 * last)
            def _(i):
                k, e = i // 2, i % 2
                step = step_of(k)
                weights = down_w[e, quarter((z + step) % SIDE), :]
                part[k, e, rows, :] = nt_dot(in_rows[rows, :width], weights).astype(jnp.bfloat16)

        products(0, 1, lambda k: 2)
        along_z(part.at[0, 0, rows], rs_far.at[0, rows], rs_send, rs_far_recv.at[c, 0], up)
        along_z(part.at[0, 1, rows], rs_far.at[1, rows], rs_send, rs_far_recv.at[c, 1], down)
        products(1, 3, lambda k: 2 * k - 1)
        along_z(part.at[1, 1, rows], rs_near.at[0, 1, rows], rs_send, rs_near_recv.at[c, 0, 1], up)
        along_z(
            part.at[2, 0, rows], rs_near.at[1, 0, rows], rs_send, rs_near_recv.at[c, 1, 0], down
        )
        products(3, 4, lambda k: 0)

    def add_far(c):
        rows = pl.ds(starts[c], sizes[c])
        for way, local in ((0, up), (1, down)):
            landed(rs_far.at[way, rows], rs_far_recv.at[c, way])
            part[1 + way, way, rows, :] = (
                part[1 + way, way, rows, :].astype(jnp.float32)
                + rs_far[way, rows, :].astype(jnp.float32)
            ).astype(jnp.bfloat16)
            along_z(
                part.at[1 + way, way, rows],
                rs_near.at[way, way, rows],
                rs_send,
                rs_near_recv.at[c, way, way],
                local,
            )

    def hidden_grads(c):
        begin, count = starts[c], sizes[c]
        rows = pl.ds(begin, count)
        for way in range(2):
            for e in range(2):
                landed(rs_near.at[way, e, rows], rs_near_recv.at[c, way, e])
        if c == 0:
            loads[1].wait()
            loads[2].wait()
        mine_columns = quarter(z)

        @pl.loop(begin // UNIT, (begin + count) // UNIT)
        def _(u):
            here = rows_of(u * UNIT, UNIT)
            saved = rows_of(node_minus(u % 16) * CAP + u // 16 * UNIT, UNIT)
            masses = in_rows[here, width:].astype(jnp.float32)
            expert = lax.broadcasted_iota(jnp.int32, (UNIT, EXTRA), 1)
            extra = jnp.zeros((UNIT, EXTRA), jnp.float32)
            for e in range(2):
                raw = (
                    part[3, e, here, :].astype(jnp.float32)
                    + rs_near[0, e, here, :].astype(jnp.float32)
                    + rs_near[1, e, here, :].astype(jnp.float32)
                )
                gate = gate_pre[e, saved, :].astype(jnp.float32)
                value = up_pre[e, saved, :].astype(jnp.float32)
                weight = jnp.sum(
                    jnp.where(expert == 2 * n + e, masses, 0.0), axis=1, keepdims=True
                )
                q = jax.nn.sigmoid(gate)
                active = gate * q
                prob = jnp.sum(raw * active * value, axis=1, keepdims=True)
                high = prob.astype(jnp.bfloat16).astype(jnp.float32)
                extra = jnp.where(expert == 2 * n + e, high, extra)
                extra = jnp.where(expert == 32 + 2 * n + e, prob - high, extra)
                scaled = raw * weight
                grads[2 * e, here, mine_columns] = (
                    scaled * value * q * (1.0 + gate * (1.0 - q))
                ).astype(jnp.bfloat16)
                grads[2 * e + 1, here, mine_columns] = (scaled * active).astype(jnp.bfloat16)
            ret_rows[here, width:] = extra.astype(jnp.bfloat16)

        for turn in range(2):
            for way, local in ((0, up), (1, down)):
                e = way ^ turn
                piece = grads.at[pl.ds(2 * e, 2), rows, mine_columns]
                along_z(piece, piece, ag_send, ag_recv.at[c, way, e], local)

    def send_on(c):
        rows = pl.ds(starts[c], sizes[c])
        for way, local, owner in ((0, up, down), (1, down, up)):
            piece = grads.at[pl.ds(2 * way, 2), rows, quarter(owner)]
            landed(piece, ag_recv.at[c, way, way])
            along_z(piece, piece, ag_send, ag_far_recv.at[c, way], local)

    def multiply_up(c):
        begin, count = starts[c], sizes[c]
        rows = pl.ds(begin, count)
        far = lax.rem(z + 2, SIDE)
        for way, owner in ((0, down), (1, up)):
            e = 1 - way
            landed(grads.at[pl.ds(2 * e, 2), rows, quarter(owner)], ag_recv.at[c, way, e])
            landed(grads.at[pl.ds(2 * way, 2), rows, quarter(far)], ag_far_recv.at[c, way])
        if c == 0:
            loads[3].wait()
            loads[4].wait()

        @pl.loop(0, width // 256)
        def _(i):
            features = pl.ds(pl.multiple_of(i * 256, 256), 256)
            ret_rows[rows, features] = (
                nt_dot(grads[0, rows, :], gate_w[0, features, :])
                + nt_dot(grads[1, rows, :], up_w[0, features, :])
                + nt_dot(grads[2, rows, :], gate_w[1, features, :])
                + nt_dot(grads[3, rows, :], up_w[1, features, :])
            ).astype(jnp.bfloat16)

        @pl.loop(begin // UNIT, (begin + count) // UNIT)
        def _(u):
            here = rows_of(u * UNIT, UNIT)
            pltpu.make_async_remote_copy(
                src_ref=ret_rows.at[here],
                dst_ref=back_rows.at[here],
                send_sem=ret_send,
                recv_sem=ret_recv.at[u // 8],
                device_id={"section": other, "node": node_minus(u % 16), "local": z},
                device_id_type=MESH,
            ).start()

    def combine(c):
        begin, count = starts[c], sizes[c]
        if c == 0:
            sel_copy.wait_recv()
        for t in range(begin // TILE, (begin + count) // TILE):
            rows = pl.ds(t * TILE, TILE)
            landed(back_rows.at[rows], ret_recv.at[t])

            @pl.loop(0, full // 384)
            def _(i):
                features = pl.ds(pl.multiple_of(i * 384, 128), 384)
                term = jnp.dot(
                    sel_other[t], back_rows[rows, features], preferred_element_type=jnp.float32
                )
                if t == 0:
                    acc[:, features] = term
                else:
                    acc[:, features] += term

    last = len(CHUNKS) - 1
    multiply_down(0)
    add_far(0)
    hidden_grads(0)
    for c in range(last + 1):
        if c > 0:
            if c < last:
                multiply_down(c + 1)
            hidden_grads(c)
        else:
            multiply_down(1)
        if c < last:
            add_far(c + 1)
        if c > 0:
            multiply_up(c - 1)
        send_on(c)
        if c > 1:
            combine(c - 2)
    multiply_up(last)
    combine(last - 1)
    combine(last)

    mine[...] = acc[:, width:]

    def hand_over(k):
        return pltpu.make_async_remote_copy(
            src_ref=mine,
            dst_ref=total.at[k],
            send_sem=tok_send.at[k],
            recv_sem=tok_recv.at[k],
            device_id={"section": other, "node": n, "local": (z + k) % SIDE},
            device_id_type=MESH,
        )

    for k in range(SIDE):
        hand_over(k).start()
    handed_ref[...] = acc[:, :width].astype(jnp.bfloat16)

    remote = rows_node - rows_node // NODES
    landed(out_rows.at[pl.ds(0, remote)], disp_send)
    sel_copy.wait_send()
    landed(part.at[pl.ds(0, 3)], rs_send)
    landed(grads.at[pl.ds(0, 3)], ag_send)
    landed(ret_rows, ret_send)

    for k in range(SIDE):
        hand_over(k).wait()
    sums = total[0] + total[1] + total[2] + total[3]
    for k in range(prob_ref.shape[1]):
        chosen = experts_ref[:, k : k + 1]
        wanted = (lane == chosen) | (lane == chosen + 32)
        value = jnp.sum(jnp.where(wanted, sums, 0.0), axis=1, keepdims=True)
        prob_ref[:, k : k + 1] = value.astype(jnp.bfloat16).astype(jnp.float32)


def shards(*args):
    grad_out, node_ids, expert_ids, gate_probs, gate_pre, up_pre, gate_w, up_w, down_w = args
    tokens, width = grad_out.shape
    full = width + EXTRA
    rows = gate_pre.shape[1]
    hidden = gate_pre.shape[2]
    chunks = len(CHUNKS)
    half, single = jnp.bfloat16, jnp.float32
    dma = pltpu.SemaphoreType.DMA
    in_vmem = pl.BlockSpec(memory_space=pltpu.VMEM)
    anywhere = pl.BlockSpec(memory_space=pl.ANY)
    return pl.pallas_call(
        kernel,
        out_shape=(
            jax.ShapeDtypeStruct((tokens, width), half),
            jax.ShapeDtypeStruct(gate_probs.shape, single),
        ),
        in_specs=[in_vmem] * 4 + [anywhere] * 5,
        out_specs=(in_vmem, in_vmem),
        scratch_shapes=[
            pltpu.VMEM(gate_pre.shape, half),
            pltpu.VMEM(up_pre.shape, half),
            pltpu.VMEM(gate_w.shape, half),
            pltpu.VMEM(up_w.shape, half),
            pltpu.VMEM(down_w.shape, half),
            pltpu.VMEM((tokens, full), half),
            pltpu.VMEM((rows // TILE, tokens, TILE), half),
            pltpu.VMEM((rows // TILE, tokens, TILE), half),
            pltpu.VMEM((rows, full), half),
            pltpu.VMEM((rows, full), half),
            pltpu.VMEM((4, 2, rows, hidden), half),
            pltpu.VMEM((2, rows, hidden), half),
            pltpu.VMEM((2, 2, rows, hidden), half),
            pltpu.VMEM((4, rows, SIDE * hidden), half),
            pltpu.VMEM((rows, full), half),
            pltpu.VMEM((rows, full), half),
            pltpu.VMEM((tokens, full), single),
            pltpu.VMEM((tokens, EXTRA), single),
            pltpu.VMEM((SIDE, tokens, EXTRA), single),
            dma((5,)),
            dma,
            dma((rows // TILE,)),
            dma,
            dma,
            dma,
            dma((chunks, 2)),
            dma((chunks, 2, 2)),
            dma,
            dma((chunks, 2, 2)),
            dma((chunks, 2)),
            dma,
            dma((rows // TILE,)),
            dma((SIDE,)),
            dma((SIDE,)),
        ],
        compiler_params=pltpu.CompilerParams(
            collective_id=0, has_side_effects=True, vmem_limit_bytes=62 * 1024 * 1024
        ),
    )(*args)


def solution(mesh):
    return jax.shard_map(
        shards,
        mesh=mesh,
        in_specs=(
            P(("section", "node"), "local"),
            P(("section", "node"), None),
            P(("section", "node"), None),
            P(("section", "node"), None),
            P(("section", "node"), None, "local"),
            P(("section", "node"), None, "local"),
            P(("section", "node"), "local", None),
            P(("section", "node"), "local", None),
            P(("section", "node"), None, "local"),
        ),
        out_specs=(P(("section", "node"), "local"), P(("section", "node"), None)),
        check_vma=False,
    )
```

```python
import functools

import jax
import jax.numpy as jnp
from jax import lax
from jax.experimental import pallas as pl
from jax.experimental.pallas import tpu as pltpu
from jax.sharding import PartitionSpec as P

MESH = pl.DeviceIdType.MESH
SIDE = 4
NODES = 16
CAP = 64
UNIT = 16
TILE = 128
BLOCK = 256
GROUP = 4
EXTRA = 128
EXPERTS = 32
CHUNKS = (8, 8, 16, 16, 8, 8)


def offset(o):
    half = o // 8
    rest = o % 8
    dy = rest // 2
    dx = (2 * (rest % 2) + dy % 2 + half) % SIDE
    return dy, dx


def nt_dot(a, b):
    return lax.dot_general(a, b, (((1,), (1,)), ((), ())), preferred_element_type=jnp.float32)


def silu_backward(raw, weight, gate, value):
    gate = gate.astype(jnp.float32)
    value = value.astype(jnp.float32)
    q = jax.nn.sigmoid(gate)
    active = gate * q
    scaled = raw * weight
    gate_grad = scaled * value * q * (1.0 + gate * (1.0 - q))
    return raw * active * value, gate_grad.astype(jnp.bfloat16), (scaled * active).astype(jnp.bfloat16)


def kernel(
    x_ref,
    nodes_ref,
    experts_ref,
    probs_ref,
    gate_pre_ref,
    up_pre_ref,
    gate_w_ref,
    up_w_ref,
    down_w_ref,
    handed_ref,
    prob_ref,
    gate_pre,
    up_pre,
    gate_w,
    up_w,
    down_w,
    table,
    x_ext,
    sel,
    sel_other,
    out_rows,
    in_rows,
    part,
    rs_far,
    rs_near,
    pre_full,
    raw_full,
    grads,
    late,
    ret_rows,
    back_rows,
    ret_prob,
    back_prob,
    acc,
    mine,
    total,
    load_sem,
    disp_send,
    disp_recv,
    sel_send,
    sel_recv,
    rs_send,
    rs_far_recv,
    rs_near_recv,
    pre_send,
    pre_recv,
    pre_far_recv,
    raw_send,
    ag_send,
    ag_recv,
    ag_far_recv,
    ret_send,
    ret_recv,
    prob_send,
    prob_recv,
    tok_send,
    tok_recv,
):
    s = lax.axis_index("section")
    n = lax.axis_index("node")
    z = lax.axis_index("local")
    other = 1 - s
    my, mx = n // SIDE, n % SIDE
    up = lax.rem(z + 1, SIDE)
    down = lax.rem(z + 3, SIDE)
    tokens, width = x_ref.shape
    rows_node = gate_pre.shape[1]
    hidden = gate_pre.shape[2]
    tiles = rows_node // TILE

    def node_plus(o):
        dy, dx = offset(o)
        return ((my + dy) % SIDE) * SIDE + (mx + dx) % SIDE

    def node_minus(o):
        dy, dx = offset(o)
        return ((my + SIDE - dy) % SIDE) * SIDE + (mx + SIDE - dx) % SIDE

    def rows_of(start, count):
        return pl.ds(start if isinstance(start, int) else pl.multiple_of(start, UNIT), count)

    def quarter(index):
        return pl.ds(pl.multiple_of(index * hidden, hidden), hidden)

    def landed(ref, sem):
        pltpu.make_async_copy(ref, ref, sem).wait()

    def send(src, dst, send_sem, recv_sem, section, node, local):
        pltpu.make_async_remote_copy(
            src_ref=src,
            dst_ref=dst,
            send_sem=send_sem,
            recv_sem=recv_sem,
            device_id={"section": section, "node": node, "local": local},
            device_id_type=MESH,
        ).start()

    def along_z(src, dst, send_sem, recv_sem, local):
        send(src, dst, send_sem, recv_sem, s, n, local)

    loads = [
        pltpu.make_async_copy(src, dst, load_sem.at[i])
        for i, (src, dst) in enumerate(
            (
                (gate_pre_ref, gate_pre),
                (up_pre_ref, up_pre),
                (down_w_ref, down_w),
                (gate_w_ref, gate_w),
                (up_w_ref, up_w),
            )
        )
    ]
    for load in loads:
        load.start()

    barrier = pltpu.get_barrier_semaphore()

    def greet(section, node, local):
        pl.semaphore_signal(
            barrier,
            inc=1,
            device_id={"section": section, "node": node, "local": local},
            device_id_type=MESH,
        )

    greet(s, n, up)
    greet(s, n, down)
    for k in range(1, SIDE):
        greet(other, n, (z + k) % SIDE)

    @pl.loop(1, NODES)
    def _(o):
        greet(s, node_plus(o), z)

    @pl.loop(0, NODES)
    def _(o):
        greet(other, node_plus(o), z)

    table[...] = jnp.zeros_like(table)
    table[0 : nodes_ref.shape[0], :] = nodes_ref[...].astype(jnp.float32)
    table[8 : 8 + experts_ref.shape[0], :] = experts_ref[...].astype(jnp.float32)
    table[16 : 16 + probs_ref.shape[0], :] = probs_ref[...]
    table[...] = table[...].T
    lane = lax.broadcasted_iota(jnp.int32, (tokens, EXTRA), 1).astype(jnp.float32)
    mass = jnp.zeros((tokens, EXTRA), jnp.float32)
    for k in range(experts_ref.shape[0]):
        mass = mass + jnp.where(
            lane == table[:, 8 + k : 9 + k], table[:, 16 + k : 17 + k], 0.0
        )
    x_ext[:, width:] = mass.astype(jnp.bfloat16)
    x_ext[:, :width] = x_ref[...]
    before = (
        lax.broadcasted_iota(jnp.int32, (tokens, tokens), 1)
        < lax.broadcasted_iota(jnp.int32, (tokens, tokens), 0)
    )
    before = jnp.where(before, 1.0, 0.0).astype(jnp.bfloat16)

    def pick(t):
        column = lax.broadcasted_iota(jnp.int32, (tokens, TILE), 1) + t * TILE
        u = column >> 4
        o = u & 15
        rest = o & 7
        dy = rest >> 1
        dx = (2 * (rest & 1) + (dy & 1) + (o >> 3)) & 3
        node = (((my + dy) & 3) * SIDE + ((mx + dx) & 3)).astype(jnp.float32)
        slot = ((u >> 4) * UNIT + (column & 15)).astype(jnp.float32)
        member = table[:, 0:1] == node
        for k in range(1, nodes_ref.shape[0]):
            member = member | (table[:, k : k + 1] == node)
        member = jnp.where(member, 1.0, 0.0)
        position = jnp.dot(
            before, member.astype(jnp.bfloat16), preferred_element_type=jnp.float32
        )
        chosen = jnp.where(position == slot, member, 0.0)
        half = t % 2 * TILE
        if not isinstance(t, int):
            half = pl.multiple_of(half, TILE)
        sel[t // 2, :, pl.ds(half, TILE)] = chosen.astype(jnp.bfloat16)
        out_rows[rows_of(t * TILE, TILE), :] = jnp.dot(
            chosen.T.astype(jnp.bfloat16), x_ext[...], preferred_element_type=jnp.float32
        ).astype(jnp.bfloat16)

    pick(0)
    pl.semaphore_wait(barrier, 2 + (SIDE - 1) + (NODES - 1) + NODES)

    starts = [UNIT * sum(CHUNKS[:c]) for c in range(len(CHUNKS))]
    sizes = [UNIT * count for count in CHUNKS]
    last = len(CHUNKS) - 1
    first_units = CHUNKS[0]

    def saved_rows(u):
        return rows_of(node_minus(u % 16) * CAP + u // 16 * UNIT, UNIT)

    def gather(ref, planes, rows, send_sem, recv_sem):
        for turn in range(2):
            for way, local in ((0, up), (1, down)):
                e = way ^ turn
                piece = ref.at[pl.ds(planes * e, planes), rows, quarter(z)]
                along_z(piece, piece, send_sem, recv_sem.at[way, e], local)

    def gather_on(ref, planes, rows, send_sem, recv_sem, far_sem):
        for way, local, owner in ((0, up, down), (1, down, up)):
            piece = ref.at[pl.ds(planes * way, planes), rows, quarter(owner)]
            landed(piece, recv_sem.at[way, way])
            along_z(piece, piece, send_sem, far_sem.at[way], local)

    def gather_near(ref, planes, rows, recv_sem):
        for way, owner in ((0, down), (1, up)):
            e = 1 - way
            landed(ref.at[pl.ds(planes * e, planes), rows, quarter(owner)], recv_sem.at[way, e])

    def gather_far(ref, planes, rows, far_sem):
        far = lax.rem(z + 2, SIDE)
        for way in range(2):
            landed(ref.at[pl.ds(planes * way, planes), rows, quarter(far)], far_sem.at[way])

    @pl.loop(0, tiles)
    def _(t):
        @pl.when(t % 2 == 0)
        def _():
            rows = rows_of(t * TILE, UNIT)
            in_rows[rows, :] = out_rows[rows, :]

        @pl.loop(1 - t % 2, TILE // UNIT)
        def _(i):
            rows = rows_of(t * TILE + i * UNIT, UNIT)
            send(
                out_rows.at[rows],
                in_rows.at[rows],
                disp_send,
                disp_recv.at[t],
                s,
                node_plus((t % 2) * 8 + i),
                z,
            )

        @pl.when(t == 0)
        def _():
            loads[0].wait()
            loads[1].wait()

            @pl.loop(0, first_units)
            def _(u):
                here, saved = rows_of(u * UNIT, UNIT), saved_rows(u)
                for e in range(2):
                    pre_full[2 * e, here, quarter(z)] = gate_pre[e, saved, :]
                    pre_full[2 * e + 1, here, quarter(z)] = up_pre[e, saved, :]

            gather(pre_full, 2, pl.ds(0, sizes[0]), pre_send, pre_recv)

        @pl.when(t + 1 < tiles)
        def _():
            pick(t + 1)

    gather_on(pre_full, 2, pl.ds(0, sizes[0]), pre_send, pre_recv, pre_far_recv)
    sel_copy = pltpu.make_async_remote_copy(
        src_ref=sel,
        dst_ref=sel_other,
        send_sem=sel_send,
        recv_sem=sel_recv,
        device_id={"section": other, "node": n, "local": z},
        device_id_type=MESH,
    )
    sel_copy.start()

    def multiply_down(c):
        begin, count = starts[c], sizes[c]
        rows = pl.ds(begin, count)
        for t in range(begin // TILE, (begin + count) // TILE):
            skip = UNIT if t % 2 == 0 else 0
            landed(in_rows.at[pl.ds(t * TILE + skip, TILE - skip)], disp_recv.at[t])
        if c == 0:
            loads[2].wait()

        def products(first, stop, step_of):
            @pl.loop(2 * first, 2 * stop)
            def _(i):
                k, e = i // 2, i % 2
                step = step_of(k)
                weights = down_w[e, quarter((z + step) % SIDE), :]
                part[k, e, rows, :] = nt_dot(in_rows[rows, :width], weights).astype(jnp.bfloat16)

        products(0, 1, lambda k: 2)
        along_z(part.at[0, 0, rows], rs_far.at[0, rows], rs_send, rs_far_recv.at[c, 0], up)
        along_z(part.at[0, 1, rows], rs_far.at[1, rows], rs_send, rs_far_recv.at[c, 1], down)
        products(1, 3, lambda k: 2 * k - 1)
        along_z(part.at[1, 1, rows], rs_near.at[0, 1, rows], rs_send, rs_near_recv.at[c, 0, 1], up)
        along_z(
            part.at[2, 0, rows], rs_near.at[1, 0, rows], rs_send, rs_near_recv.at[c, 1, 0], down
        )
        products(3, 4, lambda k: 0)

    def add_far(c):
        rows = pl.ds(starts[c], sizes[c])
        for way, local in ((0, up), (1, down)):
            landed(rs_far.at[way, rows], rs_far_recv.at[c, way])
            part[1 + way, way, rows, :] = (
                part[1 + way, way, rows, :].astype(jnp.float32)
                + rs_far[way, rows, :].astype(jnp.float32)
            ).astype(jnp.bfloat16)
            along_z(
                part.at[1 + way, way, rows],
                rs_near.at[way, way, rows],
                rs_send,
                rs_near_recv.at[c, way, way],
                local,
            )

    def expert_weight(here, e):
        masses = in_rows[here, width:].astype(jnp.float32)
        expert = lax.broadcasted_iota(jnp.int32, masses.shape, 1)
        return jnp.sum(jnp.where(expert == 2 * n + e, masses, 0.0), axis=1, keepdims=True)

    def hidden_grads(c):
        begin, count = starts[c], sizes[c]
        rows = pl.ds(begin, count)
        for way in range(2):
            for e in range(2):
                landed(rs_near.at[way, e, rows], rs_near_recv.at[c, way, e])
        step = GROUP * UNIT

        @pl.loop(begin // step, (begin + count) // step)
        def _(g):
            here = rows_of(g * step, step)
            expert = lax.broadcasted_iota(jnp.int32, (step, EXTRA), 1)
            extra = jnp.zeros((step, EXTRA), jnp.float32)
            saved = [saved_rows(g * GROUP + i) for i in range(GROUP)]
            for e in range(2):
                raw = (
                    part[3, e, here, :].astype(jnp.float32)
                    + rs_near[0, e, here, :].astype(jnp.float32)
                    + rs_near[1, e, here, :].astype(jnp.float32)
                )
                terms, gate_grad, up_grad = silu_backward(
                    raw,
                    expert_weight(here, e),
                    jnp.concatenate([gate_pre[e, one, :] for one in saved], axis=0),
                    jnp.concatenate([up_pre[e, one, :] for one in saved], axis=0),
                )
                prob = jnp.sum(terms, axis=1, keepdims=True)
                high = prob.astype(jnp.bfloat16).astype(jnp.float32)
                extra = jnp.where(expert == 2 * n + e, high, extra)
                extra = jnp.where(expert == EXPERTS + 2 * n + e, prob - high, extra)
                grads[2 * e, here, quarter(z)] = gate_grad
                grads[2 * e + 1, here, quarter(z)] = up_grad
                if c == 0:
                    raw_full[e, here, quarter(z)] = raw.astype(jnp.bfloat16)
            ret_prob[here, :] = extra.astype(jnp.bfloat16)

        if c == 0:
            gather(raw_full, 1, rows, raw_send, ag_recv.at[c])
        else:
            gather(grads, 2, rows, ag_send, ag_recv.at[c])

        @pl.loop(begin // UNIT, (begin + count) // UNIT)
        def _(u):
            here = rows_of(u * UNIT, UNIT)
            send(
                ret_prob.at[here],
                back_prob.at[here],
                prob_send,
                prob_recv,
                other,
                node_minus(u % 16),
                z,
            )

    def send_on(c):
        rows = pl.ds(starts[c], sizes[c])
        if c == 0:
            gather_on(raw_full, 1, rows, raw_send, ag_recv.at[c], ag_far_recv.at[c])
        else:
            gather_on(grads, 2, rows, ag_send, ag_recv.at[c], ag_far_recv.at[c])

    def send_back(c, features):
        @pl.loop(starts[c] // UNIT, (starts[c] + sizes[c]) // UNIT)
        def _(u):
            here = rows_of(u * UNIT, UNIT)
            send(
                ret_rows.at[here, features],
                back_rows.at[here, features],
                ret_send,
                ret_recv.at[u // 16],
                other,
                node_minus(u % 16),
                z,
            )

    def feature_tile(i):
        return pl.ds(pl.multiple_of(i * 256, 256), 256)

    def up_product(rows, features, columns):
        return (
            nt_dot(grads[0, rows, columns], gate_w[0, features, columns])
            + nt_dot(grads[1, rows, columns], up_w[0, features, columns])
            + nt_dot(grads[2, rows, columns], gate_w[1, features, columns])
            + nt_dot(grads[3, rows, columns], up_w[1, features, columns])
        )

    def multiply_up(c):
        rows = pl.ds(starts[c], sizes[c])
        if c == 0:
            gather_near(raw_full, 1, rows, ag_recv.at[c])
            gather_far(raw_full, 1, rows, ag_far_recv.at[c])
            gather_near(pre_full, 2, rows, pre_recv)
            gather_far(pre_full, 2, rows, pre_far_recv)
            step = GROUP * UNIT
            groups = sizes[0] // step

            @pl.loop(0, (SIDE - 1) * groups)
            def _(i):
                here = rows_of(i % groups * step, step)
                columns = quarter((z + 1 + i // groups) % SIDE)
                for e in range(2):
                    _, gate_grad, up_grad = silu_backward(
                        raw_full[e, here, columns].astype(jnp.float32),
                        expert_weight(here, e),
                        pre_full[2 * e, here, columns],
                        pre_full[2 * e + 1, here, columns],
                    )
                    grads[2 * e, here, columns] = gate_grad
                    grads[2 * e + 1, here, columns] = up_grad

            loads[3].wait()
            loads[4].wait()
        else:
            gather_near(grads, 2, rows, ag_recv.at[c])
            gather_far(grads, 2, rows, ag_far_recv.at[c])

        @pl.loop(0, width // 256)
        def _(i):
            features = feature_tile(i)
            ret_rows[rows, features] = up_product(rows, features, pl.ds(0, SIDE * hidden)).astype(
                jnp.bfloat16
            )

        send_back(c, pl.ds(0, width))

    def multiply_up_near(c):
        rows = pl.ds(starts[c], sizes[c])
        gather_near(grads, 2, rows, ag_recv.at[c])

        @pl.loop(0, width // 256)
        def _(i):
            features = feature_tile(i)
            late[:, features] = (
                up_product(rows, features, quarter(z))
                + up_product(rows, features, quarter(up))
                + up_product(rows, features, quarter(down))
            )

    def multiply_up_far(c):
        rows = pl.ds(starts[c], sizes[c])
        gather_far(grads, 2, rows, ag_far_recv.at[c])
        columns = quarter(lax.rem(z + 2, SIDE))
        cut = width // 256 // 2 + 1
        for first, stop in ((0, cut), (cut, width // 256)):

            @pl.loop(first, stop)
            def _(i):
                features = feature_tile(i)
                ret_rows[rows, features] = (
                    late[:, features] + up_product(rows, features, columns)
                ).astype(jnp.bfloat16)

            send_back(c, pl.ds(first * 256, (stop - first) * 256))

    def combine(b):
        rows = pl.ds(b * BLOCK, BLOCK)
        landed(back_rows.at[rows], ret_recv.at[b])

        @pl.loop(0, width // 256)
        def _(i):
            features = feature_tile(i)
            term = jnp.dot(
                sel_other[b], back_rows[rows, features], preferred_element_type=jnp.float32
            )
            if b == 0:
                acc[:, features] = term
            elif b < rows_node // BLOCK - 1:
                acc[:, features] += term
            else:
                handed_ref[:, features] = (acc[:, features] + term).astype(jnp.bfloat16)

    def hand_over(k):
        return pltpu.make_async_remote_copy(
            src_ref=mine,
            dst_ref=total.at[k],
            send_sem=tok_send.at[k],
            recv_sem=tok_recv.at[k],
            device_id={"section": other, "node": n, "local": (z + k) % SIDE},
            device_id_type=MESH,
        )

    multiply_down(0)
    add_far(0)
    hidden_grads(0)
    multiply_down(1)
    send_on(0)
    add_far(1)
    for c in range(1, last + 1):
        if c < last:
            multiply_down(c + 1)
        hidden_grads(c)
        if c < last:
            add_far(c + 1)
        multiply_up(c - 1)
        send_on(c)
        if c == 4:
            sel_copy.wait_recv()
            combine(0)
        if c == 5:
            combine(1)
    multiply_up_near(last)
    landed(back_prob, prob_recv)
    tokens_prob = jnp.zeros((tokens, EXTRA), jnp.float32)
    for b in range(rows_node // BLOCK):
        tokens_prob = tokens_prob + jnp.dot(
            sel_other[b],
            back_prob[b * BLOCK : (b + 1) * BLOCK, :],
            preferred_element_type=jnp.float32,
        )
    mine[...] = tokens_prob
    for k in range(SIDE):
        hand_over(k).start()
    combine(2)
    multiply_up_far(last)

    for k in range(SIDE):
        hand_over(k).wait()
    sums = (total[0] + total[1] + total[2] + total[3]).T
    sums = sums[:EXPERTS] + sums[EXPERTS : 2 * EXPERTS]
    expert = lax.broadcasted_iota(jnp.int32, (EXPERTS, tokens), 0)
    for k in range(prob_ref.shape[0]):
        value = jnp.sum(
            jnp.where(expert == experts_ref[k : k + 1, :], sums, 0.0), axis=0, keepdims=True
        )
        prob_ref[k : k + 1, :] = value.astype(jnp.bfloat16).astype(jnp.float32)

    landed(out_rows.at[pl.ds(0, rows_node - rows_node // NODES)], disp_send)
    sel_copy.wait_send()
    landed(part.at[pl.ds(0, 3)], rs_send)
    landed(pre_full.at[pl.ds(0, 3)], pre_send)
    landed(raw_full.at[:, :, pl.ds(0, 3 * hidden)], raw_send)
    landed(grads.at[pl.ds(0, 3), pl.ds(0, rows_node - sizes[0])], ag_send)
    landed(ret_prob, prob_send)
    landed(ret_rows, ret_send)
    combine(3)


def shards(*args):
    grad_out, node_ids, expert_ids, gate_probs, gate_pre, up_pre, gate_w, up_w, down_w = args
    tokens, width = grad_out.shape
    full = width + EXTRA
    rows = gate_pre.shape[1]
    hidden = gate_pre.shape[2]
    chunks = len(CHUNKS)
    first = UNIT * CHUNKS[0]
    half, single = jnp.bfloat16, jnp.float32
    dma = pltpu.SemaphoreType.DMA
    in_vmem = pl.BlockSpec(memory_space=pltpu.VMEM)
    anywhere = pl.BlockSpec(memory_space=pl.ANY)
    results = (
        pltpu.VMEM((tokens, width), half),
        pltpu.VMEM(gate_probs.shape[::-1], single),
    )
    handed, prob = pl.pallas_call(
        kernel,
        out_shape=results,
        in_specs=[in_vmem] * 4 + [anywhere] * 5,
        out_specs=(in_vmem, in_vmem),
        scratch_shapes=[
            pltpu.VMEM(gate_pre.shape, half),
            pltpu.VMEM(up_pre.shape, half),
            pltpu.VMEM(gate_w.shape, half),
            pltpu.VMEM(up_w.shape, half),
            pltpu.VMEM(down_w.shape, half),
            pltpu.VMEM((tokens, tokens), single),
            pltpu.VMEM((tokens, full), half),
            pltpu.VMEM((rows // BLOCK, tokens, BLOCK), half),
            pltpu.VMEM((rows // BLOCK, tokens, BLOCK), half),
            pltpu.VMEM((rows, full), half),
            pltpu.VMEM((rows, full), half),
            pltpu.VMEM((4, 2, rows, hidden), half),
            pltpu.VMEM((2, rows, hidden), half),
            pltpu.VMEM((2, 2, rows, hidden), half),
            pltpu.VMEM((4, first, SIDE * hidden), half),
            pltpu.VMEM((2, first, SIDE * hidden), half),
            pltpu.VMEM((4, rows, SIDE * hidden), half),
            pltpu.VMEM((UNIT * CHUNKS[-1], width), single),
            pltpu.VMEM((rows, width), half),
            pltpu.VMEM((rows, width), half),
            pltpu.VMEM((rows, EXTRA), half),
            pltpu.VMEM((rows, EXTRA), half),
            pltpu.VMEM((tokens, width), single),
            pltpu.VMEM((tokens, EXTRA), single),
            pltpu.VMEM((SIDE, tokens, EXTRA), single),
            dma((5,)),
            dma,
            dma((rows // TILE,)),
            dma,
            dma,
            dma,
            dma((chunks, 2)),
            dma((chunks, 2, 2)),
            dma,
            dma((2, 2)),
            dma((2,)),
            dma,
            dma,
            dma((chunks, 2, 2)),
            dma((chunks, 2)),
            dma,
            dma((rows // BLOCK,)),
            dma,
            dma,
            dma((SIDE,)),
            dma((SIDE,)),
        ],
        compiler_params=pltpu.CompilerParams(
            collective_id=0, has_side_effects=True, vmem_limit_bytes=62 * 1024 * 1024
        ),
    )(
        grad_out,
        node_ids.T,
        expert_ids.T,
        gate_probs.T,
        gate_pre,
        up_pre,
        gate_w,
        up_w,
        down_w,
    )
    return handed, prob.T


def solution(mesh):
    return jax.shard_map(
        shards,
        mesh=mesh,
        in_specs=(
            P(("section", "node"), "local"),
            P(("section", "node"), None),
            P(("section", "node"), None),
            P(("section", "node"), None),
            P(("section", "node"), None, "local"),
            P(("section", "node"), None, "local"),
            P(("section", "node"), "local", None),
            P(("section", "node"), "local", None),
            P(("section", "node"), None, "local"),
        ),
        out_specs=(P(("section", "node"), "local"), P(("section", "node"), None)),
        check_vma=False,
    )
```

```python
import jax
import jax.numpy as jnp
from jax import lax
from jax.experimental import pallas as pl
from jax.experimental.pallas import tpu as pltpu
from jax.sharding import PartitionSpec as P

MESH = pl.DeviceIdType.MESH
SIDE = 4
NODES = 16
CAP = 64
UNIT = 16
TILE = 128
BLOCK = 256
GROUP = 4
EXTRA = 128
EXPERTS = 32
CHUNKS = (8, 8, 8, 8, 8, 8, 8, 8)


def near(u):
    i = u % 4
    return u // 4 % 4, i // 2 * (1 + 2 * (i % 2)), (1 - i // 2) * (1 + 2 * (i % 2))


def near_last(u):
    return 3, *near(u)[1:]


def straight(u):
    return (u - 12) // 2, 2 * (u % 2), 2 * (1 - u % 2)


def diagonal(u):
    place = 4 * ((u - 20) % 9) % 9
    return (u - 20) // 9, 1 + place // 3, 1 + place % 3


def home(u):
    return u - 60, 0, 0


RANGES = ((0, 12, near), (12, 20, straight), (20, 56, diagonal), (56, 60, near_last), (60, 64, home))


def ranges(begin, stop):
    for low, high, place in RANGES:
        if max(begin, low) < min(stop, high):
            yield max(begin, low), min(stop, high), place


def nt_dot(a, b):
    return lax.dot_general(a, b, (((1,), (1,)), ((), ())), preferred_element_type=jnp.float32)


def silu_backward(raw, weight, gate, value):
    gate = gate.astype(jnp.float32)
    value = value.astype(jnp.float32)
    q = jax.nn.sigmoid(gate)
    active = gate * q
    scaled = raw * weight
    gate_grad = scaled * value * q * (1.0 + gate * (1.0 - q))
    return raw * active * value, gate_grad.astype(jnp.bfloat16), (scaled * active).astype(jnp.bfloat16)


def kernel(
    x_ref,
    nodes_ref,
    experts_ref,
    probs_ref,
    gate_pre_ref,
    up_pre_ref,
    gate_w_ref,
    up_w_ref,
    down_w_ref,
    handed_ref,
    prob_ref,
    gate_pre,
    up_pre,
    gate_w,
    up_w,
    down_w,
    table,
    column_node,
    column_slot,
    x_ext,
    sel,
    sel_other,
    out_rows,
    in_rows,
    part,
    rs_far,
    rs_near,
    pre_full,
    raw_full,
    grads,
    late,
    ret_rows,
    back_rows,
    ret_prob,
    back_prob,
    acc,
    mine,
    total,
    load_sem,
    disp_send,
    disp_recv,
    sel_send,
    sel_recv,
    rs_send,
    rs_far_recv,
    rs_near_recv,
    pre_send,
    pre_recv,
    pre_far_recv,
    raw_send,
    ag_send,
    ag_recv,
    ag_far_recv,
    ret_send,
    ret_recv,
    prob_send,
    prob_recv,
    tok_send,
    tok_recv,
):
    s = lax.axis_index("section")
    n = lax.axis_index("node")
    z = lax.axis_index("local")
    other = 1 - s
    my, mx = n // SIDE, n % SIDE
    up = lax.rem(z + 1, SIDE)
    down = lax.rem(z + 3, SIDE)
    tokens, width = x_ref.shape
    rows_node = gate_pre.shape[1]
    hidden = gate_pre.shape[2]
    tiles = rows_node // TILE

    def node_plus(dy, dx):
        return ((my + dy) % SIDE) * SIDE + (mx + dx) % SIDE

    def node_minus(dy, dx):
        return ((my + SIDE - dy) % SIDE) * SIDE + (mx + SIDE - dx) % SIDE

    def rows_of(start, count):
        return pl.ds(start if isinstance(start, int) else pl.multiple_of(start, UNIT), count)

    def quarter(index):
        return pl.ds(pl.multiple_of(index * hidden, hidden), hidden)

    def landed(ref, sem):
        pltpu.make_async_copy(ref, ref, sem).wait()

    def send(src, dst, send_sem, recv_sem, section, node, local):
        pltpu.make_async_remote_copy(
            src_ref=src,
            dst_ref=dst,
            send_sem=send_sem,
            recv_sem=recv_sem,
            device_id={"section": section, "node": node, "local": local},
            device_id_type=MESH,
        ).start()

    def along_z(src, dst, send_sem, recv_sem, local):
        send(src, dst, send_sem, recv_sem, s, n, local)

    loads = [
        pltpu.make_async_copy(src, dst, load_sem.at[i])
        for i, (src, dst) in enumerate(
            (
                (gate_pre_ref, gate_pre),
                (up_pre_ref, up_pre),
                (down_w_ref, down_w),
                (gate_w_ref, gate_w),
                (up_w_ref, up_w),
            )
        )
    ]
    for load in loads:
        load.start()

    barrier = pltpu.get_barrier_semaphore()

    def greet(section, node, local):
        pl.semaphore_signal(
            barrier,
            inc=1,
            device_id={"section": section, "node": node, "local": local},
            device_id_type=MESH,
        )

    greet(s, n, up)
    greet(s, n, down)
    for k in range(1, SIDE):
        greet(other, n, (z + k) % SIDE)

    @pl.loop(1, NODES)
    def _(o):
        greet(s, node_plus(o // SIDE, o % SIDE), z)

    @pl.loop(0, NODES)
    def _(o):
        greet(other, node_plus(o // SIDE, o % SIDE), z)

    table[...] = jnp.zeros_like(table)
    table[0 : nodes_ref.shape[0], :] = nodes_ref[...].astype(jnp.float32)
    table[8 : 8 + experts_ref.shape[0], :] = experts_ref[...].astype(jnp.float32)
    table[16 : 16 + probs_ref.shape[0], :] = probs_ref[...]
    table[...] = table[...].T
    lane = lax.broadcasted_iota(jnp.int32, (tokens, EXTRA), 1).astype(jnp.float32)
    mass = jnp.zeros((tokens, EXTRA), jnp.float32)
    for k in range(experts_ref.shape[0]):
        mass = mass + jnp.where(
            lane == table[:, 8 + k : 9 + k], table[:, 16 + k : 17 + k], 0.0
        )
    x_ext[:, width:] = mass.astype(jnp.bfloat16)
    x_ext[:, :width] = x_ref[...]
    before = (
        lax.broadcasted_iota(jnp.int32, (tokens, tokens), 1)
        < lax.broadcasted_iota(jnp.int32, (tokens, tokens), 0)
    )
    before = jnp.where(before, 1.0, 0.0).astype(jnp.bfloat16)

    unit_of_lane = lax.broadcasted_iota(jnp.int32, (1, TILE), 1) // UNIT
    slot_of_lane = lax.broadcasted_iota(jnp.int32, (1, TILE), 1) % UNIT
    for t in range(tiles):
        node = jnp.zeros((1, TILE), jnp.int32)
        slot = slot_of_lane
        for i in range(TILE // UNIT):
            u = t * (TILE // UNIT) + i
            place = next(f for low, high, f in RANGES if low <= u < high)
            q, dy, dx = place(u)
            node = jnp.where(unit_of_lane == i, node_plus(dy, dx), node)
            slot = slot + jnp.where(unit_of_lane == i, q * UNIT, 0)
        column_node[t : t + 1, :] = node.astype(jnp.float32)
        column_slot[t : t + 1, :] = slot.astype(jnp.float32)

    def pick(t):
        node = column_node[t : t + 1, :]
        member = table[:, 0:1] == node
        for k in range(1, nodes_ref.shape[0]):
            member = member | (table[:, k : k + 1] == node)
        member = jnp.where(member, 1.0, 0.0)
        position = jnp.dot(
            before, member.astype(jnp.bfloat16), preferred_element_type=jnp.float32
        )
        chosen = jnp.where(position == column_slot[t : t + 1, :], member, 0.0)
        sel[t // 2, :, t % 2 * TILE : (t % 2 + 1) * TILE] = chosen.astype(jnp.bfloat16)
        picked = chosen.T.astype(jnp.bfloat16)

        @pl.loop(0, x_ext.shape[1] // 384)
        def _(i):
            features = pl.ds(pl.multiple_of(i * 384, 128), 384)
            out_rows[t * TILE : (t + 1) * TILE, features] = jnp.dot(
                picked, x_ext[:, features], preferred_element_type=jnp.float32
            ).astype(jnp.bfloat16)

    pick(0)
    pl.semaphore_wait(barrier, 2 + (SIDE - 1) + (NODES - 1) + NODES)

    starts = [UNIT * sum(CHUNKS[:c]) for c in range(len(CHUNKS))]
    sizes = [UNIT * count for count in CHUNKS]
    last = len(CHUNKS) - 1
    first_units = CHUNKS[0]

    def saved_rows(q, dy, dx):
        return rows_of(node_minus(dy, dx) * CAP + q * UNIT, UNIT)

    def gather(ref, planes, rows, send_sem, recv_sem):
        for turn in range(2):
            for way, local in ((0, up), (1, down)):
                e = way ^ turn
                piece = ref.at[pl.ds(planes * e, planes), rows, quarter(z)]
                along_z(piece, piece, send_sem, recv_sem.at[way, e], local)

    def gather_on(ref, planes, rows, send_sem, recv_sem, far_sem):
        for way, local, owner in ((0, up, down), (1, down, up)):
            piece = ref.at[pl.ds(planes * way, planes), rows, quarter(owner)]
            landed(piece, recv_sem.at[way, way])
            along_z(piece, piece, send_sem, far_sem.at[way], local)

    def gather_near(ref, planes, rows, recv_sem):
        for way, owner in ((0, down), (1, up)):
            e = 1 - way
            landed(ref.at[pl.ds(planes * e, planes), rows, quarter(owner)], recv_sem.at[way, e])

    def gather_far(ref, planes, rows, far_sem):
        far = lax.rem(z + 2, SIDE)
        for way in range(2):
            landed(ref.at[pl.ds(planes * way, planes), rows, quarter(far)], far_sem.at[way])

    def send_rows(t):
        if t > 0:
            pick(t)
        for low, high, place in ranges(t * TILE // UNIT, (t + 1) * TILE // UNIT):
            if place is home:
                rows = pl.ds(low * UNIT, (high - low) * UNIT)
                in_rows[rows, :] = out_rows[rows, :]
                continue

            @pl.loop(low, high)
            def _(u):
                rows = rows_of(u * UNIT, UNIT)
                _, dy, dx = place(u)
                send(
                    out_rows.at[rows],
                    in_rows.at[rows],
                    disp_send,
                    disp_recv.at[t],
                    s,
                    node_plus(dy, dx),
                    z,
                )

        if t == tiles - 1:
            sel_copy().start()

    def rows_arrived(t):
        remote = sum(
            high - low
            for low, high, place in ranges(t * TILE // UNIT, (t + 1) * TILE // UNIT)
            if place is not home
        )
        landed(in_rows.at[pl.ds(t * TILE, remote * UNIT)], disp_recv.at[t])

    def sel_copy():
        return pltpu.make_async_remote_copy(
            src_ref=sel,
            dst_ref=sel_other,
            send_sem=sel_send,
            recv_sem=sel_recv,
            device_id={"section": other, "node": n, "local": z},
            device_id_type=MESH,
        )

    def gather_saved(_):
        loads[0].wait()
        loads[1].wait()
        for low, high, place in ranges(0, first_units):

            @pl.loop(low, high)
            def _(u):
                here, saved = rows_of(u * UNIT, UNIT), saved_rows(*place(u))
                for e in range(2):
                    pre_full[2 * e, here, quarter(z)] = gate_pre[e, saved, :]
                    pre_full[2 * e + 1, here, quarter(z)] = up_pre[e, saved, :]

        gather(pre_full, 2, pl.ds(0, sizes[0]), pre_send, pre_recv)

    def gather_saved_on(_):
        gather_on(pre_full, 2, pl.ds(0, sizes[0]), pre_send, pre_recv, pre_far_recv)

    def multiply_down(c):
        begin, count = starts[c], sizes[c]
        rows = pl.ds(begin, count)
        for t in range(begin // TILE, (begin + count) // TILE):
            rows_arrived(t)
        if c == 0:
            loads[2].wait()

        def products(first, stop, step_of):
            @pl.loop(2 * first, 2 * stop)
            def _(i):
                k, e = i // 2, i % 2
                step = step_of(k)
                weights = down_w[e, quarter((z + step) % SIDE), :]
                part[k, e, rows, :] = nt_dot(in_rows[rows, :width], weights).astype(jnp.bfloat16)

        products(0, 1, lambda k: 2)
        along_z(part.at[0, 0, rows], rs_far.at[0, rows], rs_send, rs_far_recv.at[c, 0], up)
        along_z(part.at[0, 1, rows], rs_far.at[1, rows], rs_send, rs_far_recv.at[c, 1], down)
        products(1, 3, lambda k: 2 * k - 1)
        along_z(part.at[1, 1, rows], rs_near.at[0, 1, rows], rs_send, rs_near_recv.at[c, 0, 1], up)
        along_z(
            part.at[2, 0, rows], rs_near.at[1, 0, rows], rs_send, rs_near_recv.at[c, 1, 0], down
        )
        products(3, 4, lambda k: 0)

    def add_far(c):
        rows = pl.ds(starts[c], sizes[c])
        for way, local in ((0, up), (1, down)):
            landed(rs_far.at[way, rows], rs_far_recv.at[c, way])
            part[1 + way, way, rows, :] = (
                part[1 + way, way, rows, :].astype(jnp.float32)
                + rs_far[way, rows, :].astype(jnp.float32)
            ).astype(jnp.bfloat16)
            along_z(
                part.at[1 + way, way, rows],
                rs_near.at[way, way, rows],
                rs_send,
                rs_near_recv.at[c, way, way],
                local,
            )

    def expert_weight(here, e):
        masses = in_rows[here, width:].astype(jnp.float32)
        expert = lax.broadcasted_iota(jnp.int32, masses.shape, 1)
        return jnp.sum(jnp.where(expert == 2 * n + e, masses, 0.0), axis=1, keepdims=True)

    def hidden_grads(c):
        begin, count = starts[c], sizes[c]
        rows = pl.ds(begin, count)
        for way in range(2):
            for e in range(2):
                landed(rs_near.at[way, e, rows], rs_near_recv.at[c, way, e])
        step = GROUP * UNIT

        def one_group(g, place):
            here = rows_of(g * step, step)
            expert = lax.broadcasted_iota(jnp.int32, (step, EXTRA), 1)
            extra = jnp.zeros((step, EXTRA), jnp.float32)
            saved = [saved_rows(*place(g * GROUP + i)) for i in range(GROUP)]
            for e in range(2):
                raw = (
                    part[3, e, here, :].astype(jnp.float32)
                    + rs_near[0, e, here, :].astype(jnp.float32)
                    + rs_near[1, e, here, :].astype(jnp.float32)
                )
                terms, gate_grad, up_grad = silu_backward(
                    raw,
                    expert_weight(here, e),
                    jnp.concatenate([gate_pre[e, one, :] for one in saved], axis=0),
                    jnp.concatenate([up_pre[e, one, :] for one in saved], axis=0),
                )
                prob = jnp.sum(terms, axis=1, keepdims=True)
                high = prob.astype(jnp.bfloat16).astype(jnp.float32)
                extra = jnp.where(expert == 2 * n + e, high, extra)
                extra = jnp.where(expert == EXPERTS + 2 * n + e, prob - high, extra)
                grads[2 * e, here, quarter(z)] = gate_grad
                grads[2 * e + 1, here, quarter(z)] = up_grad
                if c == 0:
                    raw_full[e, here, quarter(z)] = raw.astype(jnp.bfloat16)
            ret_prob[here, :] = extra.astype(jnp.bfloat16)

        for low, high, place in ranges(begin // UNIT, (begin + count) // UNIT):

            @pl.loop(low // GROUP, high // GROUP)
            def _(g):
                one_group(g, place)

        if c == 0:
            gather(raw_full, 1, rows, raw_send, ag_recv.at[c])
        else:
            gather(grads, 2, rows, ag_send, ag_recv.at[c])

        for low, high, place in ranges(begin // UNIT, (begin + count) // UNIT):

            @pl.loop(low, high)
            def _(u):
                here = rows_of(u * UNIT, UNIT)
                _, dy, dx = place(u)
                send(
                    ret_prob.at[here],
                    back_prob.at[here],
                    prob_send,
                    prob_recv,
                    other,
                    node_minus(dy, dx),
                    z,
                )

    def send_on(c):
        rows = pl.ds(starts[c], sizes[c])
        if c == 0:
            gather_on(raw_full, 1, rows, raw_send, ag_recv.at[c], ag_far_recv.at[c])
        else:
            gather_on(grads, 2, rows, ag_send, ag_recv.at[c], ag_far_recv.at[c])

    def send_back(c, features):
        for low, high, place in ranges(starts[c] // UNIT, (starts[c] + sizes[c]) // UNIT):

            @pl.loop(low, high)
            def _(u):
                here = rows_of(u * UNIT, UNIT)
                _, dy, dx = place(u)
                send(
                    ret_rows.at[here, features],
                    back_rows.at[here, features],
                    ret_send,
                    ret_recv.at[u // 16],
                    other,
                    node_minus(dy, dx),
                    z,
                )

    def feature_tile(i):
        return pl.ds(pl.multiple_of(i * 256, 256), 256)

    def up_product(rows, features, columns):
        return (
            nt_dot(grads[0, rows, columns], gate_w[0, features, columns])
            + nt_dot(grads[1, rows, columns], up_w[0, features, columns])
            + nt_dot(grads[2, rows, columns], gate_w[1, features, columns])
            + nt_dot(grads[3, rows, columns], up_w[1, features, columns])
        )

    def await_grads(c):
        rows = pl.ds(starts[c], sizes[c])
        if c == 0:
            gather_near(raw_full, 1, rows, ag_recv.at[c])
            gather_far(raw_full, 1, rows, ag_far_recv.at[c])
            gather_near(pre_full, 2, rows, pre_recv)
            gather_far(pre_full, 2, rows, pre_far_recv)
            step = GROUP * UNIT
            groups = sizes[0] // step

            @pl.loop(0, (SIDE - 1) * groups)
            def _(i):
                here = rows_of(i % groups * step, step)
                columns = quarter((z + 1 + i // groups) % SIDE)
                for e in range(2):
                    _, gate_grad, up_grad = silu_backward(
                        raw_full[e, here, columns].astype(jnp.float32),
                        expert_weight(here, e),
                        pre_full[2 * e, here, columns],
                        pre_full[2 * e + 1, here, columns],
                    )
                    grads[2 * e, here, columns] = gate_grad
                    grads[2 * e + 1, here, columns] = up_grad

            loads[3].wait()
            loads[4].wait()
        else:
            gather_near(grads, 2, rows, ag_recv.at[c])
            gather_far(grads, 2, rows, ag_far_recv.at[c])

    cut = width // 256 // 2 + 1

    def multiply_up(c, first, stop):
        rows = pl.ds(starts[c], sizes[c])

        @pl.loop(first, stop)
        def _(i):
            features = feature_tile(i)
            ret_rows[rows, features] = up_product(rows, features, pl.ds(0, SIDE * hidden)).astype(
                jnp.bfloat16
            )

        send_back(c, pl.ds(first * 256, (stop - first) * 256))

    def multiply_up_low(c):
        await_grads(c)
        multiply_up(c, 0, cut)

    def multiply_up_high(c):
        multiply_up(c, cut, width // 256)

    def multiply_up_own(c):
        rows = pl.ds(starts[c], sizes[c])

        @pl.loop(0, width // 256)
        def _(i):
            features = feature_tile(i)
            late[:, features] = up_product(rows, features, quarter(z))

    def multiply_up_near(c):
        rows = pl.ds(starts[c], sizes[c])
        gather_near(grads, 2, rows, ag_recv.at[c])

        @pl.loop(0, width // 256)
        def _(i):
            features = feature_tile(i)
            late[:, features] += up_product(rows, features, quarter(up)) + up_product(
                rows, features, quarter(down)
            )

    def multiply_up_far(c):
        rows = pl.ds(starts[c], sizes[c])
        gather_far(grads, 2, rows, ag_far_recv.at[c])
        columns = quarter(lax.rem(z + 2, SIDE))
        for first, stop in ((0, cut), (cut, width // 256)):

            @pl.loop(first, stop)
            def _(i):
                features = feature_tile(i)
                ret_rows[rows, features] = (
                    late[:, features] + up_product(rows, features, columns)
                ).astype(jnp.bfloat16)

            send_back(c, pl.ds(first * 256, (stop - first) * 256))

    def combine(b):
        rows = pl.ds(b * BLOCK, BLOCK)
        if b == 0:
            sel_copy().wait_recv()
        landed(back_rows.at[rows], ret_recv.at[b])

        @pl.loop(0, width // 256)
        def _(i):
            features = feature_tile(i)
            term = jnp.dot(
                sel_other[b], back_rows[rows, features], preferred_element_type=jnp.float32
            )
            if b == 0:
                acc[:, features] = term
            elif b < rows_node // BLOCK - 1:
                acc[:, features] += term
            else:
                handed_ref[:, features] = (acc[:, features] + term).astype(jnp.bfloat16)

    def hand_over(k):
        return pltpu.make_async_remote_copy(
            src_ref=mine,
            dst_ref=total.at[k],
            send_sem=tok_send.at[k],
            recv_sem=tok_recv.at[k],
            device_id={"section": other, "node": n, "local": (z + k) % SIDE},
            device_id_type=MESH,
        )

    def sum_prob(_):
        landed(back_prob, prob_recv)
        tokens_prob = jnp.zeros((tokens, EXTRA), jnp.float32)
        for b in range(rows_node // BLOCK):
            tokens_prob = tokens_prob + jnp.dot(
                sel_other[b],
                back_prob[b * BLOCK : (b + 1) * BLOCK, :],
                preferred_element_type=jnp.float32,
            )
        mine[...] = tokens_prob
        for k in range(SIDE):
            hand_over(k).start()

    for step, index in (
        (send_rows, 0),
        (gather_saved, 0),
        (send_rows, 1),
        (send_rows, 2),
        (send_rows, 3),
        (send_rows, 4),
        (multiply_down, 0),
        (gather_saved_on, 0),
        (add_far, 0),
        (multiply_down, 1),
        (send_rows, 5),
        (hidden_grads, 0),
        (multiply_down, 2),
        (add_far, 1),
        (send_on, 0),
        (multiply_down, 3),
        (hidden_grads, 1),
        (add_far, 2),
        (multiply_up_low, 0),
        (add_far, 3),
        (send_on, 1),
        (multiply_down, 4),
        (hidden_grads, 2),
        (multiply_down, 5),
        (send_rows, 6),
        (multiply_up_high, 0),
        (add_far, 4),
        (send_on, 2),
        (hidden_grads, 3),
        (send_rows, 7),
        (multiply_up_low, 1),
        (multiply_up_high, 1),
        (hidden_grads, 4),
        (add_far, 5),
        (multiply_up_low, 2),
        (send_on, 3),
        (multiply_down, 6),
        (multiply_down, 7),
        (multiply_up_high, 2),
        (send_on, 4),
        (hidden_grads, 5),
        (multiply_up_low, 3),
        (multiply_up_high, 3),
        (add_far, 6),
        (multiply_up_low, 4),
        (send_on, 5),
        (add_far, 7),
        (multiply_up_high, 4),
        (hidden_grads, 6),
        (combine, 0),
        (multiply_up_low, 5),
        (send_on, 6),
        (hidden_grads, 7),
        (multiply_up_own, 7),
        (multiply_up_high, 5),
        (multiply_up_low, 6),
        (send_on, 7),
        (multiply_up_high, 6),
        (multiply_up_near, 7),
        (sum_prob, 0),
        (multiply_up_far, 7),
        (combine, 1),
        (combine, 2),
    ):
        step(index)

    for k in range(SIDE):
        hand_over(k).wait()
    sums = (total[0] + total[1] + total[2] + total[3]).T
    sums = sums[:EXPERTS] + sums[EXPERTS : 2 * EXPERTS]
    expert = lax.broadcasted_iota(jnp.int32, (EXPERTS, tokens), 0)
    for k in range(prob_ref.shape[0]):
        value = jnp.sum(
            jnp.where(expert == experts_ref[k : k + 1, :], sums, 0.0), axis=0, keepdims=True
        )
        prob_ref[k : k + 1, :] = value.astype(jnp.bfloat16).astype(jnp.float32)

    landed(out_rows.at[pl.ds(0, rows_node - rows_node // NODES)], disp_send)
    sel_copy().wait_send()
    landed(part.at[pl.ds(0, 3)], rs_send)
    landed(pre_full.at[pl.ds(0, 3)], pre_send)
    landed(raw_full.at[:, :, pl.ds(0, 3 * hidden)], raw_send)
    landed(grads.at[pl.ds(0, 3), pl.ds(0, rows_node - sizes[0])], ag_send)
    landed(ret_prob, prob_send)
    landed(ret_rows, ret_send)
    combine(3)


def shards(*args):
    grad_out, node_ids, expert_ids, gate_probs, gate_pre, up_pre, gate_w, up_w, down_w = args
    tokens, width = grad_out.shape
    full = width + EXTRA
    rows = gate_pre.shape[1]
    hidden = gate_pre.shape[2]
    chunks = len(CHUNKS)
    first = UNIT * CHUNKS[0]
    half, single = jnp.bfloat16, jnp.float32
    dma = pltpu.SemaphoreType.DMA
    in_vmem = pl.BlockSpec(memory_space=pltpu.VMEM)
    anywhere = pl.BlockSpec(memory_space=pl.ANY)
    results = (
        pltpu.VMEM((tokens, width), half),
        pltpu.VMEM(gate_probs.shape[::-1], single),
    )
    handed, prob = pl.pallas_call(
        kernel,
        out_shape=results,
        in_specs=[in_vmem] * 4 + [anywhere] * 5,
        out_specs=(in_vmem, in_vmem),
        scratch_shapes=[
            pltpu.VMEM(gate_pre.shape, half),
            pltpu.VMEM(up_pre.shape, half),
            pltpu.VMEM(gate_w.shape, half),
            pltpu.VMEM(up_w.shape, half),
            pltpu.VMEM(down_w.shape, half),
            pltpu.VMEM((tokens, tokens), single),
            pltpu.VMEM((rows // TILE, TILE), single),
            pltpu.VMEM((rows // TILE, TILE), single),
            pltpu.VMEM((tokens, full), half),
            pltpu.VMEM((rows // BLOCK, tokens, BLOCK), half),
            pltpu.VMEM((rows // BLOCK, tokens, BLOCK), half),
            pltpu.VMEM((rows, full), half),
            pltpu.VMEM((rows, full), half),
            pltpu.VMEM((4, 2, rows, hidden), half),
            pltpu.VMEM((2, rows, hidden), half),
            pltpu.VMEM((2, 2, rows, hidden), half),
            pltpu.VMEM((4, first, SIDE * hidden), half),
            pltpu.VMEM((2, first, SIDE * hidden), half),
            pltpu.VMEM((4, rows, SIDE * hidden), half),
            pltpu.VMEM((UNIT * CHUNKS[-1], width), single),
            pltpu.VMEM((rows, width), half),
            pltpu.VMEM((rows, width), half),
            pltpu.VMEM((rows, EXTRA), half),
            pltpu.VMEM((rows, EXTRA), half),
            pltpu.VMEM((tokens, width), single),
            pltpu.VMEM((tokens, EXTRA), single),
            pltpu.VMEM((SIDE, tokens, EXTRA), single),
            dma((5,)),
            dma,
            dma((rows // TILE,)),
            dma,
            dma,
            dma,
            dma((chunks, 2)),
            dma((chunks, 2, 2)),
            dma,
            dma((2, 2)),
            dma((2,)),
            dma,
            dma,
            dma((chunks, 2, 2)),
            dma((chunks, 2)),
            dma,
            dma((rows // BLOCK,)),
            dma,
            dma,
            dma((SIDE,)),
            dma((SIDE,)),
        ],
        compiler_params=pltpu.CompilerParams(
            collective_id=0, has_side_effects=True, vmem_limit_bytes=62 * 1024 * 1024
        ),
    )(
        grad_out,
        node_ids.T,
        expert_ids.T,
        gate_probs.T,
        gate_pre,
        up_pre,
        gate_w,
        up_w,
        down_w,
    )
    return handed, prob.T


def solution(mesh):
    return jax.shard_map(
        shards,
        mesh=mesh,
        in_specs=(
            P(("section", "node"), "local"),
            P(("section", "node"), None),
            P(("section", "node"), None),
            P(("section", "node"), None),
            P(("section", "node"), None, "local"),
            P(("section", "node"), None, "local"),
            P(("section", "node"), "local", None),
            P(("section", "node"), "local", None),
            P(("section", "node"), None, "local"),
        ),
        out_specs=(P(("section", "node"), "local"), P(("section", "node"), None)),
        check_vma=False,
    )
```

```python
import jax
import jax.numpy as jnp
from jax import lax
from jax.experimental import pallas as pl
from jax.experimental.pallas import tpu as pltpu
from jax.sharding import PartitionSpec as P

MESH = pl.DeviceIdType.MESH
SIDE = 4
NODES = 16
CAP = 64
UNIT = 16
TILE = 128
BLOCK = 256
GROUP = 4
EXTRA = 128
EXPERTS = 32
CHUNKS = (8, 8, 8, 8, 8, 8, 8, 8)
DOWN_GROUPS = ((0,), (1,), (2,), (3, 4), (5, 6), (7,))
UP_GROUPS = ((0, 1), (2, 3), (4, 5), (6,))


def near(u):
    i = u % 4
    return u // 4 % 4, i // 2 * (1 + 2 * (i % 2)), (1 - i // 2) * (1 + 2 * (i % 2))


def near_last(u):
    return 3, *near(u)[1:]


def straight(u):
    return (u - 12) // 2, 2 * (u % 2), 2 * (1 - u % 2)


def diagonal(u):
    place = 4 * ((u - 20) % 9) % 9
    return (u - 20) // 9, 1 + place // 3, 1 + place % 3


def home(u):
    return u - 60, 0, 0


RANGES = ((0, 12, near), (12, 20, straight), (20, 56, diagonal), (56, 60, near_last), (60, 64, home))


def ranges(begin, stop):
    for low, high, place in RANGES:
        if max(begin, low) < min(stop, high):
            yield max(begin, low), min(stop, high), place


def nt_dot(a, b):
    return lax.dot_general(a, b, (((1,), (1,)), ((), ())), preferred_element_type=jnp.float32)


def silu_backward(raw, weight, gate, value):
    gate = gate.astype(jnp.float32)
    value = value.astype(jnp.float32)
    q = jax.nn.sigmoid(gate)
    active = gate * q
    scaled = raw * weight
    gate_grad = scaled * value * q * (1.0 + gate * (1.0 - q))
    return raw * active * value, gate_grad.astype(jnp.bfloat16), (scaled * active).astype(jnp.bfloat16)


def kernel(
    x_hbm,
    nodes_hbm,
    experts_hbm,
    probs_hbm,
    gate_pre_ref,
    up_pre_ref,
    gate_w_ref,
    up_w_ref,
    down_w_ref,
    handed_ref,
    prob_ref,
    gate_pre,
    up_pre,
    gate_w,
    up_w,
    down_w,
    nodes_ref,
    experts_ref,
    probs_ref,
    table,
    column_node,
    column_slot,
    x_ext,
    sel,
    sel_other,
    out_rows,
    in_rows,
    part,
    rs_far,
    rs_near,
    pre_full,
    raw_full,
    grads,
    late,
    ret_rows,
    back_rows,
    ret_prob,
    back_prob,
    acc,
    mine,
    total,
    load_sem,
    disp_send,
    disp_recv,
    sel_send,
    sel_recv,
    rs_send,
    rs_far_recv,
    rs_near_recv,
    pre_send,
    pre_recv,
    pre_far_recv,
    raw_send,
    ag_send,
    ag_recv,
    ag_far_recv,
    ret_send,
    ret_recv,
    prob_send,
    prob_recv,
    tok_send,
    tok_recv,
):
    s = lax.axis_index("section")
    n = lax.axis_index("node")
    z = lax.axis_index("local")
    other = 1 - s
    my, mx = n // SIDE, n % SIDE
    up = lax.rem(z + 1, SIDE)
    down = lax.rem(z + 3, SIDE)
    tokens, width = x_hbm.shape
    rows_node = gate_pre.shape[1]
    hidden = gate_pre.shape[2]
    tiles = rows_node // TILE

    def node_plus(dy, dx):
        return ((my + dy) % SIDE) * SIDE + (mx + dx) % SIDE

    def node_minus(dy, dx):
        return ((my + SIDE - dy) % SIDE) * SIDE + (mx + SIDE - dx) % SIDE

    def rows_of(start, count):
        return pl.ds(start if isinstance(start, int) else pl.multiple_of(start, UNIT), count)

    def quarter(index):
        return pl.ds(pl.multiple_of(index * hidden, hidden), hidden)

    def landed(ref, sem):
        pltpu.make_async_copy(ref, ref, sem).wait()

    def send(src, dst, send_sem, recv_sem, section, node, local):
        pltpu.make_async_remote_copy(
            src_ref=src,
            dst_ref=dst,
            send_sem=send_sem,
            recv_sem=recv_sem,
            device_id={"section": section, "node": node, "local": local},
            device_id_type=MESH,
        ).start()

    def along_z(src, dst, send_sem, recv_sem, local):
        send(src, dst, send_sem, recv_sem, s, n, local)

    loads = [
        pltpu.make_async_copy(src, dst, load_sem.at[i])
        for i, (src, dst) in enumerate(
            (
                (gate_pre_ref, gate_pre),
                (up_pre_ref, up_pre),
                (down_w_ref, down_w),
                (gate_w_ref, gate_w),
                (up_w_ref, up_w),
                (nodes_hbm, nodes_ref),
                (experts_hbm, experts_ref),
                (probs_hbm, probs_ref),
                (x_hbm, x_ext.at[:, pl.ds(0, width)]),
            )
        )
    ]
    for load in loads[5:]:
        load.start()

    barrier = pltpu.get_barrier_semaphore()

    def greet(section, node, local):
        pl.semaphore_signal(
            barrier,
            inc=1,
            device_id={"section": section, "node": node, "local": local},
            device_id_type=MESH,
        )

    greet(s, n, up)
    greet(s, n, down)
    for k in range(1, SIDE):
        greet(other, n, (z + k) % SIDE)

    @pl.loop(1, NODES)
    def _(o):
        greet(s, node_plus(o // SIDE, o % SIDE), z)

    @pl.loop(0, NODES)
    def _(o):
        greet(other, node_plus(o // SIDE, o % SIDE), z)

    for load in loads[:5]:
        load.start()
    for load in loads[5:]:
        load.wait()

    table[...] = jnp.zeros_like(table)
    table[0 : nodes_ref.shape[0], :] = nodes_ref[...].astype(jnp.float32)
    table[8 : 8 + experts_ref.shape[0], :] = experts_ref[...].astype(jnp.float32)
    table[16 : 16 + probs_ref.shape[0], :] = probs_ref[...]
    table[...] = table[...].T
    lane = lax.broadcasted_iota(jnp.int32, (tokens, EXTRA), 1).astype(jnp.float32)
    mass = jnp.zeros((tokens, EXTRA), jnp.float32)
    for k in range(experts_ref.shape[0]):
        mass = mass + jnp.where(
            lane == table[:, 8 + k : 9 + k], table[:, 16 + k : 17 + k], 0.0
        )
    x_ext[:, width:] = mass.astype(jnp.bfloat16)
    before = (
        lax.broadcasted_iota(jnp.int32, (tokens, tokens), 1)
        < lax.broadcasted_iota(jnp.int32, (tokens, tokens), 0)
    )
    before = jnp.where(before, 1.0, 0.0).astype(jnp.bfloat16)

    unit_of_lane = lax.broadcasted_iota(jnp.int32, (1, TILE), 1) // UNIT
    slot_of_lane = lax.broadcasted_iota(jnp.int32, (1, TILE), 1) % UNIT
    for t in range(tiles):
        node = jnp.zeros((1, TILE), jnp.int32)
        slot = slot_of_lane
        for i in range(TILE // UNIT):
            u = t * (TILE // UNIT) + i
            place = next(f for low, high, f in RANGES if low <= u < high)
            q, dy, dx = place(u)
            node = jnp.where(unit_of_lane == i, node_plus(dy, dx), node)
            slot = slot + jnp.where(unit_of_lane == i, q * UNIT, 0)
        column_node[t : t + 1, :] = node.astype(jnp.float32)
        column_slot[t : t + 1, :] = slot.astype(jnp.float32)

    def pick(t):
        node = column_node[t : t + 1, :]
        member = table[:, 0:1] == node
        for k in range(1, nodes_ref.shape[0]):
            member = member | (table[:, k : k + 1] == node)
        member = jnp.where(member, 1.0, 0.0)
        position = jnp.dot(
            before, member.astype(jnp.bfloat16), preferred_element_type=jnp.float32
        )
        chosen = jnp.where(position == column_slot[t : t + 1, :], member, 0.0)
        sel[t // 2, :, t % 2 * TILE : (t % 2 + 1) * TILE] = chosen.astype(jnp.bfloat16)
        out_rows[t * TILE : (t + 1) * TILE, :] = jnp.dot(
            chosen.T.astype(jnp.bfloat16), x_ext[...], preferred_element_type=jnp.float32
        ).astype(jnp.bfloat16)

    pick(0)
    pl.semaphore_wait(barrier, 2 + (SIDE - 1) + (NODES - 1) + NODES)

    starts = [UNIT * sum(CHUNKS[:c]) for c in range(len(CHUNKS))]
    sizes = [UNIT * count for count in CHUNKS]
    last = len(CHUNKS) - 1
    first_units = CHUNKS[0]

    def saved_rows(q, dy, dx):
        return rows_of(node_minus(dy, dx) * CAP + q * UNIT, UNIT)

    def gather(ref, planes, rows, send_sem, recv_sem):
        for turn in range(2):
            for way, local in ((0, up), (1, down)):
                e = way ^ turn
                piece = ref.at[pl.ds(planes * e, planes), rows, quarter(z)]
                along_z(piece, piece, send_sem, recv_sem.at[way, e], local)

    def gather_on(ref, planes, rows, send_sem, recv_sem, far_sem):
        for way, local, owner in ((0, up, down), (1, down, up)):
            piece = ref.at[pl.ds(planes * way, planes), rows, quarter(owner)]
            landed(piece, recv_sem.at[way, way])
            along_z(piece, piece, send_sem, far_sem.at[way], local)

    def gather_near(ref, planes, rows, recv_sem):
        for way, owner in ((0, down), (1, up)):
            e = 1 - way
            landed(ref.at[pl.ds(planes * e, planes), rows, quarter(owner)], recv_sem.at[way, e])

    def gather_far(ref, planes, rows, far_sem):
        far = lax.rem(z + 2, SIDE)
        for way in range(2):
            landed(ref.at[pl.ds(planes * way, planes), rows, quarter(far)], far_sem.at[way])

    def send_rows(t):
        if t > 0:
            pick(t)
        for low, high, place in ranges(t * TILE // UNIT, (t + 1) * TILE // UNIT):
            if place is home:
                rows = pl.ds(low * UNIT, (high - low) * UNIT)
                in_rows[rows, :] = out_rows[rows, :]
                continue

            @pl.loop(low, high)
            def _(u):
                rows = rows_of(u * UNIT, UNIT)
                _, dy, dx = place(u)
                send(
                    out_rows.at[rows],
                    in_rows.at[rows],
                    disp_send,
                    disp_recv.at[t],
                    s,
                    node_plus(dy, dx),
                    z,
                )

        if t == tiles - 1:
            sel_copy().start()

    def rows_arrived(t):
        remote = sum(
            high - low
            for low, high, place in ranges(t * TILE // UNIT, (t + 1) * TILE // UNIT)
            if place is not home
        )
        landed(in_rows.at[pl.ds(t * TILE, remote * UNIT)], disp_recv.at[t])

    def sel_copy():
        return pltpu.make_async_remote_copy(
            src_ref=sel,
            dst_ref=sel_other,
            send_sem=sel_send,
            recv_sem=sel_recv,
            device_id={"section": other, "node": n, "local": z},
            device_id_type=MESH,
        )

    def gather_saved(_):
        loads[0].wait()
        loads[1].wait()
        for low, high, place in ranges(0, first_units):

            @pl.loop(low, high)
            def _(u):
                here, saved = rows_of(u * UNIT, UNIT), saved_rows(*place(u))
                for e in range(2):
                    pre_full[2 * e, here, quarter(z)] = gate_pre[e, saved, :]
                    pre_full[2 * e + 1, here, quarter(z)] = up_pre[e, saved, :]

        gather(pre_full, 2, pl.ds(0, sizes[0]), pre_send, pre_recv)

    def gather_saved_on(_):
        gather_on(pre_full, 2, pl.ds(0, sizes[0]), pre_send, pre_recv, pre_far_recv)

    def chunk_rows(c):
        return pl.ds(starts[c], sizes[c])

    def multiply_down(g):
        chunks = DOWN_GROUPS[g]
        begin, count = starts[chunks[0]], sum(sizes[c] for c in chunks)
        rows = pl.ds(begin, count)
        for t in range(begin // TILE, (begin + count) // TILE):
            rows_arrived(t)
        if g == 0:
            loads[2].wait()

        def products(first, stop, step_of):
            @pl.loop(2 * first, 2 * stop)
            def _(i):
                k, e = i // 2, i % 2
                step = step_of(k)
                weights = down_w[e, quarter((z + step) % SIDE), :]
                part[k, e, rows, :] = nt_dot(in_rows[rows, :width], weights).astype(jnp.bfloat16)

        if g == 0:
            one = chunk_rows(0)
            for e, local in ((0, up), (1, down)):
                weights = down_w[e, quarter((z + 2) % SIDE), :]
                part[0, e, one, :] = nt_dot(in_rows[one, :width], weights).astype(jnp.bfloat16)
                along_z(part.at[0, e, one], rs_far.at[e, one], rs_send, rs_far_recv.at[0, e], local)
        else:
            products(0, 1, lambda k: 2)
        for c in chunks if g > 0 else ():
            one = chunk_rows(c)
            along_z(part.at[0, 0, one], rs_far.at[0, one], rs_send, rs_far_recv.at[c, 0], up)
            along_z(part.at[0, 1, one], rs_far.at[1, one], rs_send, rs_far_recv.at[c, 1], down)
        products(1, 3, lambda k: 2 * k - 1)
        for c in chunks:
            one = chunk_rows(c)
            along_z(
                part.at[1, 1, one], rs_near.at[0, 1, one], rs_send, rs_near_recv.at[c, 0, 1], up
            )
            along_z(
                part.at[2, 0, one], rs_near.at[1, 0, one], rs_send, rs_near_recv.at[c, 1, 0], down
            )
        products(3, 4, lambda k: 0)

    def add_far(c):
        rows = pl.ds(starts[c], sizes[c])
        for way, local in ((0, up), (1, down)):
            landed(rs_far.at[way, rows], rs_far_recv.at[c, way])
            part[1 + way, way, rows, :] = (
                part[1 + way, way, rows, :].astype(jnp.float32)
                + rs_far[way, rows, :].astype(jnp.float32)
            ).astype(jnp.bfloat16)
            along_z(
                part.at[1 + way, way, rows],
                rs_near.at[way, way, rows],
                rs_send,
                rs_near_recv.at[c, way, way],
                local,
            )

    def expert_weight(here, e):
        masses = in_rows[here, width:].astype(jnp.float32)
        expert = lax.broadcasted_iota(jnp.int32, masses.shape, 1)
        return jnp.sum(jnp.where(expert == 2 * n + e, masses, 0.0), axis=1, keepdims=True)

    def hidden_grads(c):
        begin, count = starts[c], sizes[c]
        rows = pl.ds(begin, count)
        for way in range(2):
            for e in range(2):
                landed(rs_near.at[way, e, rows], rs_near_recv.at[c, way, e])
        step = GROUP * UNIT

        def one_group(g, place):
            here = rows_of(g * step, step)
            expert = lax.broadcasted_iota(jnp.int32, (step, EXTRA), 1)
            extra = jnp.zeros((step, EXTRA), jnp.float32)
            saved = [saved_rows(*place(g * GROUP + i)) for i in range(GROUP)]
            for e in range(2):
                raw = (
                    part[3, e, here, :].astype(jnp.float32)
                    + rs_near[0, e, here, :].astype(jnp.float32)
                    + rs_near[1, e, here, :].astype(jnp.float32)
                )
                terms, gate_grad, up_grad = silu_backward(
                    raw,
                    expert_weight(here, e),
                    jnp.concatenate([gate_pre[e, one, :] for one in saved], axis=0),
                    jnp.concatenate([up_pre[e, one, :] for one in saved], axis=0),
                )
                prob = jnp.sum(terms, axis=1, keepdims=True)
                high = prob.astype(jnp.bfloat16).astype(jnp.float32)
                extra = jnp.where(expert == 2 * n + e, high, extra)
                extra = jnp.where(expert == EXPERTS + 2 * n + e, prob - high, extra)
                grads[2 * e, here, quarter(z)] = gate_grad
                grads[2 * e + 1, here, quarter(z)] = up_grad
                if c == 0:
                    raw_full[e, here, quarter(z)] = raw.astype(jnp.bfloat16)
            ret_prob[here, :] = extra.astype(jnp.bfloat16)

        for low, high, place in ranges(begin // UNIT, (begin + count) // UNIT):

            @pl.loop(low // GROUP, high // GROUP)
            def _(g):
                one_group(g, place)

        if c == 0:
            gather(raw_full, 1, rows, raw_send, ag_recv.at[c])
        else:
            gather(grads, 2, rows, ag_send, ag_recv.at[c])

        for low, high, place in ranges(begin // UNIT, (begin + count) // UNIT):

            @pl.loop(low, high)
            def _(u):
                here = rows_of(u * UNIT, UNIT)
                _, dy, dx = place(u)
                send(
                    ret_prob.at[here],
                    back_prob.at[here],
                    prob_send,
                    prob_recv,
                    other,
                    node_minus(dy, dx),
                    z,
                )

    def send_on(c):
        rows = pl.ds(starts[c], sizes[c])
        if c == 0:
            gather_on(raw_full, 1, rows, raw_send, ag_recv.at[c], ag_far_recv.at[c])
        else:
            gather_on(grads, 2, rows, ag_send, ag_recv.at[c], ag_far_recv.at[c])

    def send_back(c, features):
        for low, high, place in ranges(starts[c] // UNIT, (starts[c] + sizes[c]) // UNIT):

            @pl.loop(low, high)
            def _(u):
                here = rows_of(u * UNIT, UNIT)
                _, dy, dx = place(u)
                send(
                    ret_rows.at[here, features],
                    back_rows.at[here, features],
                    ret_send,
                    ret_recv.at[u // 16],
                    other,
                    node_minus(dy, dx),
                    z,
                )

    def feature_tile(i):
        return pl.ds(pl.multiple_of(i * 256, 256), 256)

    def up_product(rows, features, columns):
        return (
            nt_dot(grads[0, rows, columns], gate_w[0, features, columns])
            + nt_dot(grads[1, rows, columns], up_w[0, features, columns])
            + nt_dot(grads[2, rows, columns], gate_w[1, features, columns])
            + nt_dot(grads[3, rows, columns], up_w[1, features, columns])
        )

    def await_grads(c):
        rows = pl.ds(starts[c], sizes[c])
        if c == 0:
            gather_near(raw_full, 1, rows, ag_recv.at[c])
            gather_far(raw_full, 1, rows, ag_far_recv.at[c])
            gather_near(pre_full, 2, rows, pre_recv)
            gather_far(pre_full, 2, rows, pre_far_recv)
            step = GROUP * UNIT
            groups = sizes[0] // step

            @pl.loop(0, (SIDE - 1) * groups)
            def _(i):
                here = rows_of(i % groups * step, step)
                columns = quarter((z + 1 + i // groups) % SIDE)
                for e in range(2):
                    _, gate_grad, up_grad = silu_backward(
                        raw_full[e, here, columns].astype(jnp.float32),
                        expert_weight(here, e),
                        pre_full[2 * e, here, columns],
                        pre_full[2 * e + 1, here, columns],
                    )
                    grads[2 * e, here, columns] = gate_grad
                    grads[2 * e + 1, here, columns] = up_grad

            loads[3].wait()
            loads[4].wait()
        else:
            gather_near(grads, 2, rows, ag_recv.at[c])
            gather_far(grads, 2, rows, ag_far_recv.at[c])

    cut = width // 256 // 2 + 1

    def multiply_up(g, first, stop):
        chunks = UP_GROUPS[g]
        rows = pl.ds(starts[chunks[0]], sum(sizes[c] for c in chunks))

        @pl.loop(first, stop)
        def _(i):
            features = feature_tile(i)
            ret_rows[rows, features] = up_product(rows, features, pl.ds(0, SIDE * hidden)).astype(
                jnp.bfloat16
            )

        for c in chunks:
            send_back(c, pl.ds(first * 256, (stop - first) * 256))

    def multiply_up_low(g):
        for c in UP_GROUPS[g]:
            await_grads(c)
        multiply_up(g, 0, cut)

    def multiply_up_high(g):
        multiply_up(g, cut, width // 256)

    def multiply_up_own(c):
        rows = pl.ds(starts[c], sizes[c])

        @pl.loop(0, width // 256)
        def _(i):
            features = feature_tile(i)
            late[:, features] = up_product(rows, features, quarter(z))

    def multiply_up_near(c):
        rows = pl.ds(starts[c], sizes[c])
        gather_near(grads, 2, rows, ag_recv.at[c])

        @pl.loop(0, width // 256)
        def _(i):
            features = feature_tile(i)
            late[:, features] += up_product(rows, features, quarter(up)) + up_product(
                rows, features, quarter(down)
            )

    def multiply_up_far(c):
        rows = pl.ds(starts[c], sizes[c])
        gather_far(grads, 2, rows, ag_far_recv.at[c])
        columns = quarter(lax.rem(z + 2, SIDE))
        for first, stop in ((0, cut), (cut, width // 256)):

            @pl.loop(first, stop)
            def _(i):
                features = feature_tile(i)
                ret_rows[rows, features] = (
                    late[:, features] + up_product(rows, features, columns)
                ).astype(jnp.bfloat16)

            send_back(c, pl.ds(first * 256, (stop - first) * 256))

    def combine(b):
        rows = pl.ds(b * BLOCK, BLOCK)
        if b == 0:
            sel_copy().wait_recv()
        landed(back_rows.at[rows], ret_recv.at[b])

        @pl.loop(0, width // 256)
        def _(i):
            features = feature_tile(i)
            term = jnp.dot(
                sel_other[b], back_rows[rows, features], preferred_element_type=jnp.float32
            )
            if b == 0:
                acc[:, features] = term
            elif b < rows_node // BLOCK - 1:
                acc[:, features] += term
            else:
                handed_ref[:, features] = (acc[:, features] + term).astype(jnp.bfloat16)

    def hand_over(k):
        return pltpu.make_async_remote_copy(
            src_ref=mine,
            dst_ref=total.at[k],
            send_sem=tok_send.at[k],
            recv_sem=tok_recv.at[k],
            device_id={"section": other, "node": n, "local": (z + k) % SIDE},
            device_id_type=MESH,
        )

    def sum_prob(_):
        landed(back_prob, prob_recv)
        tokens_prob = jnp.zeros((tokens, EXTRA), jnp.float32)
        for b in range(rows_node // BLOCK):
            tokens_prob = tokens_prob + jnp.dot(
                sel_other[b],
                back_prob[b * BLOCK : (b + 1) * BLOCK, :],
                preferred_element_type=jnp.float32,
            )
        mine[...] = tokens_prob
        for k in range(SIDE):
            hand_over(k).start()

    for step, index in (
        (send_rows, 0),
        (gather_saved, 0),
        (send_rows, 1),
        (send_rows, 2),
        (send_rows, 3),
        (send_rows, 4),
        (gather_saved_on, 0),
        (multiply_down, 0),
        (multiply_down, 1),
        (add_far, 0),
        (add_far, 1),
        (multiply_down, 2),
        (hidden_grads, 0),
        (send_rows, 5),
        (add_far, 2),
        (send_rows, 6),
        (hidden_grads, 1),
        (hidden_grads, 2),
        (multiply_down, 3),
        (send_on, 1),
        (send_on, 0),
        (send_rows, 7),
        (add_far, 3),
        (add_far, 4),
        (multiply_down, 4),
        (hidden_grads, 3),
        (multiply_up_low, 0),
        (add_far, 5),
        (send_on, 3),
        (send_on, 2),
        (hidden_grads, 5),
        (hidden_grads, 4),
        (multiply_up_high, 0),
        (add_far, 6),
        (multiply_up_low, 1),
        (multiply_up_high, 1),
        (send_on, 5),
        (send_on, 4),
        (combine, 0),
        (multiply_down, 5),
        (hidden_grads, 6),
        (multiply_up_low, 2),
        (add_far, 7),
        (send_on, 6),
        (multiply_up_high, 2),
        (hidden_grads, 7),
        (multiply_up_own, 7),
        (multiply_up_low, 3),
        (send_on, 7),
        (multiply_up_high, 3),
        (multiply_up_near, 7),
        (multiply_up_far, 7),
        (sum_prob, 0),
        (combine, 1),
        (combine, 2),
    ):
        step(index)

    for k in range(SIDE):
        hand_over(k).wait()
    sums = (total[0] + total[1] + total[2] + total[3]).T
    sums = sums[:EXPERTS] + sums[EXPERTS : 2 * EXPERTS]
    expert = lax.broadcasted_iota(jnp.int32, (EXPERTS, tokens), 0)
    for k in range(prob_ref.shape[0]):
        value = jnp.sum(
            jnp.where(expert == experts_ref[k : k + 1, :], sums, 0.0), axis=0, keepdims=True
        )
        prob_ref[k : k + 1, :] = value.astype(jnp.bfloat16).astype(jnp.float32)

    landed(out_rows.at[pl.ds(0, rows_node - rows_node // NODES)], disp_send)
    sel_copy().wait_send()
    landed(part.at[pl.ds(0, 3)], rs_send)
    landed(pre_full.at[pl.ds(0, 3)], pre_send)
    landed(raw_full.at[:, :, pl.ds(0, 3 * hidden)], raw_send)
    landed(grads.at[pl.ds(0, 3), pl.ds(0, rows_node - sizes[0])], ag_send)
    landed(ret_prob, prob_send)
    landed(ret_rows, ret_send)
    combine(3)


def shards(*args):
    grad_out, node_ids, expert_ids, gate_probs, gate_pre, up_pre, gate_w, up_w, down_w = args
    tokens, width = grad_out.shape
    full = width + EXTRA
    rows = gate_pre.shape[1]
    hidden = gate_pre.shape[2]
    chunks = len(CHUNKS)
    first = UNIT * CHUNKS[0]
    half, single = jnp.bfloat16, jnp.float32
    dma = pltpu.SemaphoreType.DMA
    in_vmem = pl.BlockSpec(memory_space=pltpu.VMEM)
    anywhere = pl.BlockSpec(memory_space=pl.ANY)
    results = (
        pltpu.VMEM((tokens, width), half),
        pltpu.VMEM(gate_probs.shape[::-1], single),
    )
    handed, prob = pl.pallas_call(
        kernel,
        out_shape=results,
        in_specs=[anywhere] * 9,
        out_specs=(in_vmem, in_vmem),
        scratch_shapes=[
            pltpu.VMEM(gate_pre.shape, half),
            pltpu.VMEM(up_pre.shape, half),
            pltpu.VMEM(gate_w.shape, half),
            pltpu.VMEM(up_w.shape, half),
            pltpu.VMEM(down_w.shape, half),
            pltpu.VMEM(node_ids.shape[::-1], jnp.int32),
            pltpu.VMEM(expert_ids.shape[::-1], jnp.int32),
            pltpu.VMEM(gate_probs.shape[::-1], single),
            pltpu.VMEM((tokens, tokens), single),
            pltpu.VMEM((rows // TILE, TILE), single),
            pltpu.VMEM((rows // TILE, TILE), single),
            pltpu.VMEM((tokens, full), half),
            pltpu.VMEM((rows // BLOCK, tokens, BLOCK), half),
            pltpu.VMEM((rows // BLOCK, tokens, BLOCK), half),
            pltpu.VMEM((rows, full), half),
            pltpu.VMEM((rows, full), half),
            pltpu.VMEM((4, 2, rows, hidden), half),
            pltpu.VMEM((2, rows, hidden), half),
            pltpu.VMEM((2, 2, rows, hidden), half),
            pltpu.VMEM((4, first, SIDE * hidden), half),
            pltpu.VMEM((2, first, SIDE * hidden), half),
            pltpu.VMEM((4, rows, SIDE * hidden), half),
            pltpu.VMEM((UNIT * CHUNKS[-1], width), single),
            pltpu.VMEM((rows, width), half),
            pltpu.VMEM((rows, width), half),
            pltpu.VMEM((rows, EXTRA), half),
            pltpu.VMEM((rows, EXTRA), half),
            pltpu.VMEM((tokens, width), single),
            pltpu.VMEM((tokens, EXTRA), single),
            pltpu.VMEM((SIDE, tokens, EXTRA), single),
            dma((9,)),
            dma,
            dma((rows // TILE,)),
            dma,
            dma,
            dma,
            dma((chunks, 2)),
            dma((chunks, 2, 2)),
            dma,
            dma((2, 2)),
            dma((2,)),
            dma,
            dma,
            dma((chunks, 2, 2)),
            dma((chunks, 2)),
            dma,
            dma((rows // BLOCK,)),
            dma,
            dma,
            dma((SIDE,)),
            dma((SIDE,)),
        ],
        compiler_params=pltpu.CompilerParams(
            collective_id=0, has_side_effects=True, vmem_limit_bytes=62 * 1024 * 1024
        ),
    )(
        grad_out,
        node_ids.T,
        expert_ids.T,
        gate_probs.T,
        gate_pre,
        up_pre,
        gate_w,
        up_w,
        down_w,
    )
    return handed, prob.T


def solution(mesh):
    return jax.shard_map(
        shards,
        mesh=mesh,
        in_specs=(
            P(("section", "node"), "local"),
            P(("section", "node"), None),
            P(("section", "node"), None),
            P(("section", "node"), None),
            P(("section", "node"), None, "local"),
            P(("section", "node"), None, "local"),
            P(("section", "node"), "local", None),
            P(("section", "node"), "local", None),
            P(("section", "node"), None, "local"),
        ),
        out_specs=(P(("section", "node"), "local"), P(("section", "node"), None)),
        check_vma=False,
    )
```
